128 devices in a mesh: ctx: 32 (over z_hi, x, y), wt: 4 (over z_lo, core).
Axes of the slice: x: 4, y: 4, z: 4 (z_hi: 2, z_lo: 2; z = z_hi * 2 + z_lo), core: 2. Of those that a mesh axis runs over, the one named last changes fastest.
Arguments:
- hidden_in: bfloat16 [8192, 1152], P('ctx'), may hold values from -6 to 6
- cotangent: bfloat16 [8192, 1152], P('ctx'), may hold values from -6 to 6
- segment_ids: int32 [8192], replicated, may hold values from 0 to 2, as said below
- block_slot: int32 [32], replicated, may hold values from 0 to 31, each once
- w_query: bfloat16 [1152, 1024], P('ctx', 'wt'), may hold values from -0.1875 to 0.1875
- w_key: bfloat16 [1152, 256], P('ctx'), may hold values from -0.1875 to 0.1875
- w_value: bfloat16 [1152, 256], P('ctx'), may hold values from -0.1875 to 0.1875
- w_out: bfloat16 [1024, 1152], P('wt', 'ctx'), may hold values from -0.1875 to 0.1875
- w_gate: bfloat16 [1152, 6912], P('ctx', 'wt'), may hold values from -0.1875 to 0.1875
- w_up: bfloat16 [1152, 6912], P('ctx', 'wt'), may hold values from -0.1875 to 0.1875
- w_down: bfloat16 [6912, 1152], P('wt', 'ctx'), may hold values from -0.078125 to 0.078125
- gain_in: float32 [1152], replicated, may hold values from 0.1 to 1.9
- gain_query: float32 [256], replicated, may hold values from 0.1 to 1.9
- gain_key: float32 [256], replicated, may hold values from 0.1 to 1.9
- gain_attn: float32 [1152], replicated, may hold values from 0.1 to 1.9
- gain_premlp: float32 [1152], replicated, may hold values from 0.1 to 1.9
- gain_mlpout: float32 [1152], replicated, may hold values from 0.1 to 1.9
Outputs:
- mixed: bfloat16 [8192, 1152], P('ctx')
- grad_in: float32 [8192, 1152], P('ctx')
- grad_query: float32 [1152, 1024], P('ctx', 'wt')
- grad_key: float32 [1152, 256], P('ctx')
- grad_value: float32 [1152, 256], P('ctx')
- grad_out: float32 [1024, 1152], P('wt', 'ctx')
- grad_gate: float32 [1152, 6912], P('ctx', 'wt')
- grad_up: float32 [1152, 6912], P('ctx', 'wt')
- grad_down: float32 [6912, 1152], P('wt', 'ctx')
- grad_gain_in: float32 [1152], replicated
- grad_gain_query: float32 [256], replicated
- grad_gain_key: float32 [256], replicated
- grad_gain_attn: float32 [1152], replicated
- grad_gain_premlp: float32 [1152], replicated
- grad_gain_mlpout: float32 [1152], replicated
The draws below stay inside these ranges and needn't reach their ends.
Inputs may be any that keep to these rules, and one draw needn't show every extreme that they name: `segment_ids`: Non-decreasing; document 1 starts at a row from 1 to 127 and ends within the last 128 rows, documents 0 and 2 fill the rest. `block_slot`: each index of ctx once.
All inputs are finite; a program needn't handle non-finite values.
Results may differ from the reference program's by a relative error of at most 0.034.
Values may be sent and summed in bfloat16 or wider, within the bound.
No kernel may reach another device: no remote copies, remote signals or barrier semaphores. Data moves between devices by JAX's collectives and lax.ppermute only.
A program may use at most 192 MiB of HBM per device.

```python
import jax
import jax.numpy as jnp
from jax import lax

D = 1152
HEADS = 4
HD = 256
FF = 6912
TOK_DEV = 256
HALF = 128
LENGTH = 8192
N_CTX = 32


def draw_segment_ids(key, part):
    key = jax.random.fold_in(key, 7)
    first_key, second_key = jax.random.split(key)
    lead = jax.random.randint(first_key, (), 1, HALF)
    tail = jax.random.randint(second_key, (), 1, HALF)
    index = jnp.arange(LENGTH, dtype=jnp.int32)
    return ((index >= lead).astype(jnp.int32) + (index >= LENGTH - tail).astype(jnp.int32)).astype(jnp.int32)


def block_scale(stream_key, dims, cuts, least, high):
    def one(axis_at, parts):
        draws = jax.random.uniform(jax.random.fold_in(jax.random.fold_in(stream_key, 6), axis_at), (parts,), jnp.float32, least / len(cuts), high / len(cuts))
        return jnp.repeat(jnp.exp(draws), dims[axis_at] // parts).reshape((-1,) + (1,) * (len(dims) - axis_at - 1))

    level = one(*cuts[0])
    for cut in cuts[1:]:
        level = level * one(*cut)
    return level


def bell_draw(stream_key, dims, scale, limit, cuts=(), kind=jnp.bfloat16):
    entries = jax.random.normal(stream_key, dims, jnp.float32) * scale
    if len(cuts) > 0:
        entries = block_scale(stream_key, dims, cuts, -0.22, 0.18) * entries
    return jnp.clip(entries, min=-limit, max=limit).astype(kind)


def setup_inputs(seed: int = 0) -> dict:
    splits = jax.random.split(jax.random.key(seed), 18)
    return {
        "hidden_in": bell_draw(splits[0], (LENGTH, D), 1.0, 6.0, ((0, 32),)),
        "cotangent": bell_draw(splits[1], (LENGTH, D), 1.0, 6.0, ((0, 32),)),
        "segment_ids": draw_segment_ids(jax.random.fold_in(splits[17], 71), 0),
        "block_slot": jax.random.permutation(splits[3], N_CTX).astype(jnp.int32),
        "w_query": bell_draw(splits[4], (D, HEADS * HD), D ** -0.5, 0.1875, ((0, 32), (1, 4))),
        "w_key": bell_draw(splits[5], (D, HD), D ** -0.5, 0.1875, ((0, 32),)),
        "w_value": bell_draw(splits[6], (D, HD), D ** -0.5, 0.1875, ((0, 32),)),
        "w_out": bell_draw(splits[7], (HEADS * HD, D), (HEADS * HD) ** -0.5, 0.1875, ((0, 4), (1, 32))),
        "w_gate": bell_draw(splits[8], (D, FF), D ** -0.5, 0.1875, ((0, 32), (1, 4))),
        "w_up": bell_draw(splits[9], (D, FF), D ** -0.5, 0.1875, ((0, 32), (1, 4))),
        "w_down": bell_draw(splits[10], (FF, D), FF ** -0.5, 0.078125, ((0, 4), (1, 32))),
        "gain_in": jnp.clip(1.0 + 0.18 * jax.random.normal(splits[11], (D,), jnp.float32), 0.1, 1.9),
        "gain_query": jnp.clip(1.0 + 0.18 * jax.random.normal(splits[12], (HD,), jnp.float32), 0.1, 1.9),
        "gain_key": jnp.clip(1.0 + 0.18 * jax.random.normal(splits[13], (HD,), jnp.float32), 0.1, 1.9),
        "gain_attn": jnp.clip(1.0 + 0.18 * jax.random.normal(splits[14], (D,), jnp.float32), 0.1, 1.9),
        "gain_premlp": jnp.clip(1.0 + 0.18 * jax.random.normal(splits[15], (D,), jnp.float32), 0.1, 1.9),
        "gain_mlpout": jnp.clip(1.0 + 0.18 * jax.random.normal(splits[16], (D,), jnp.float32), 0.1, 1.9),
    }


@jax.custom_vjp
def low(v):
    return lax.optimization_barrier(v.astype(jnp.bfloat16)).astype(jnp.float32)

@jax.custom_vjp
def low_back(v):
    return v

def low_keep(v):
    return (low(v), None)

def low_pass(kept, grad):
    return (grad,)

def back_keep(v):
    return (v, None)

def back_low(kept, grad):
    return (low(grad),)
low.defvjp(low_keep, low_pass)
low_back.defvjp(back_keep, back_low)
EPSILON = 1e-06
THETA = 1000000.0
HIGH = lax.Precision.HIGHEST

def normed(values, gain):
    return values * lax.rsqrt(lax.optimization_barrier(jnp.mean(values * values, axis=-1, keepdims=True)) + EPSILON) * gain

def rotate(values, places, sign):
    width = values.shape[-1]
    half = width // 2
    freqs = THETA ** (-2.0 * jnp.arange(half, dtype=jnp.float32) / width)
    angles = places.astype(jnp.float32)[..., None] * freqs
    cosine = jnp.cos(angles)
    sine = sign * jnp.sin(angles)
    first = values[..., :half]
    second = values[..., half:]
    return jnp.concatenate([first * cosine - second * sine, second * cosine + first * sine], axis=-1)

def positions(segment):
    length = segment.shape[0]
    index = jnp.arange(length, dtype=jnp.int32)
    change = jnp.concatenate([jnp.ones((1,), bool), segment[1:] != segment[:-1]])
    return (index - lax.cummax(jnp.where(change, index, 0), axis=0)).astype(jnp.int32)

def dealt_rows(block_slot, tokens):
    groups = block_slot.shape[0]
    half = tokens // 2
    rows = jnp.arange(tokens, dtype=jnp.int32)
    blocks = jnp.where(rows[None, :] < half, block_slot[:, None], 2 * groups - 1 - block_slot[:, None])
    return (blocks * half + rows[None, :] % half).astype(jnp.int32)

def attend(queries, keys, values, segment):
    length = queries.shape[0]
    block = min(512, length)
    factor = queries.shape[-1] ** (-0.5)
    index = jnp.arange(length, dtype=jnp.int32)

    def one_block(item):
        query_block, query_index = item
        scores = low_back(jnp.einsum('thd,kd->thk', query_block, keys, precision=HIGH) * factor)
        allowed = (index[None, :] <= query_index[:, None]) & (segment[None, :] == segment[query_index][:, None])
        scores = jnp.where(allowed[:, None, :], scores, -1e+30)
        weights = low(jax.nn.softmax(scores, axis=-1))
        return jnp.einsum('thk,kd->thd', weights, values, precision=HIGH)
    blocks = queries.reshape(length // block, block, queries.shape[1], queries.shape[2])
    result = lax.map(jax.checkpoint(one_block), (blocks, index.reshape(length // block, block)))
    return result.reshape(queries.shape)

def forward(params, stream, places, segment):
    w_query, w_key, w_value, w_out, w_gate, w_up, w_down, gain_in, gain_query, gain_key, gain_attn, gain_premlp, gain_mlpout = params
    length = stream.shape[0]
    head_size = gain_query.shape[0]
    normed_in = low(normed(stream, gain_in))
    query_lin = low_back(jnp.dot(normed_in, w_query, precision=HIGH))
    key_lin = low_back(jnp.dot(normed_in, w_key, precision=HIGH))
    value_lin = low_back(jnp.dot(normed_in, w_value, precision=HIGH))
    queries = low(rotate(normed(query_lin.reshape(length, -1, head_size), gain_query), places[:, None], 1.0))
    keys = low(rotate(normed(key_lin, gain_key), places, 1.0))
    values = low(value_lin)
    heads = low(low_back(attend(queries, keys, values, segment))).reshape(length, -1)
    attn_out = low_back(jnp.dot(heads, w_out, precision=HIGH))
    middle = stream + normed(attn_out, gain_attn)
    normed_mid = low(normed(middle, gain_premlp))
    gate = low_back(jnp.dot(normed_mid, w_gate, precision=HIGH))
    up_proj = low_back(jnp.dot(normed_mid, w_up, precision=HIGH))
    hidden = low(jax.nn.gelu(gate, approximate=True) * up_proj)
    branch = low_back(jnp.dot(hidden, w_down, precision=HIGH))
    return middle + normed(branch, gain_mlpout)

def reference(hidden_in, cotangent, segment_ids, block_slot, w_query, w_key, w_value, w_out, w_gate, w_up, w_down, gain_in, gain_query, gain_key, gain_attn, gain_premlp, gain_mlpout):
    order = dealt_rows(block_slot, TOK_DEV).reshape(-1)
    inverse = jnp.zeros_like(order).at[order].set(jnp.arange(order.shape[0], dtype=jnp.int32))
    stream = hidden_in.astype(jnp.float32)[inverse]
    upstream = cotangent.astype(jnp.float32)[inverse]
    params = tuple((weight.astype(jnp.float32) for weight in (w_query, w_key, w_value, w_out, w_gate, w_up, w_down, gain_in, gain_query, gain_key, gain_attn, gain_premlp, gain_mlpout)))
    places = positions(segment_ids)

    def apply(weights, inputs):
        return forward(weights, inputs, places, segment_ids)
    result, pull = jax.vjp(apply, params, stream)
    totals, input_grad = pull(upstream)
    mixed = result[order].astype(jnp.bfloat16)
    grad_in = input_grad[order]
    return (mixed, grad_in, totals[0], totals[1], totals[2], totals[3], totals[4], totals[5], totals[6], totals[7], totals[8], totals[9], totals[10], totals[11], totals[12])
```

```python
import jax
import jax.numpy as jnp
import numpy as np
from jax import lax
from jax.experimental import pallas as pl
from jax.experimental.pallas import tpu as pltpu
from jax.sharding import Mesh, PartitionSpec as P

EPSILON = 1e-06
THETA = 1000000.0
HEAD = 256
HEADS = 4
WIDTH = 1152
ROWS = 36
HIDDEN = 864
WIDE = 896
OWN = 64
GROUP = 512
KEYS = 1024
RING = ("zh", "zl")
EIGHT = ("zh", "zl", "c")
PLANE = ("x", "y")
VMEM_LIMIT = 56 * 1024 * 1024

_at = np.arange(WIDTH)
INNER = ((_at // ROWS) % 2 * 16 + (_at // ROWS) // 2) * ROWS + _at % ROWS


def normalize(values, gain):
    scale_inv = lax.rsqrt(jnp.mean(values * values, axis=-1, keepdims=True) + EPSILON)
    return (values * scale_inv * gain, scale_inv)


def normalize_back(values, scale_inv, gain, upstream):
    scaled = upstream * gain
    gain_term = upstream * values * scale_inv
    inner = jnp.mean(scaled * values, axis=-1, keepdims=True)
    return (scale_inv * scaled - values * scale_inv * scale_inv * scale_inv * inner, gain_term)


def turn(values, cosine, sine):
    half = values.shape[-1] // 2
    first = values[..., :half]
    second = values[..., half:]
    return jnp.concatenate(
        [first * cosine - second * sine, second * cosine + first * sine], axis=-1
    )


def product(left, right, **kw):
    return jnp.dot(left, right, preferred_element_type=jnp.float32, **kw)


def times_transpose(left, right, **kw):
    return lax.dot_general(
        left, right, (((1,), (1,)), ((), ())), preferred_element_type=jnp.float32, **kw
    )


def left_product(left, right):
    return lax.dot_general(
        left, right, (((0,), (0,)), ((), ())), preferred_element_type=jnp.float32
    )


def low(values):
    return values.astype(jnp.bfloat16)


def split_two(values):
    high = lax.reduce_precision(values, exponent_bits=8, mantissa_bits=7)
    return (high, values - high)


def swap(values, axis):
    return lax.ppermute(values, axis, [(0, 1), (1, 0)])


def ring(values, step):
    return lax.ppermute(values, RING, [(i, (i + step) % 4) for i in range(4)])


def gather_eight(piece):
    parts = [piece] + [ring(piece, step) for step in range(1, 4)]
    parts = parts + [swap(part, "c") for part in parts]
    return jnp.concatenate(
        [part[:32] for part in parts] + [part[32:] for part in parts], axis=0
    )


def scatter_eight(partial, middle=None):
    width = partial.shape[-1]
    blocks = partial.reshape(2, 2, 128, width)
    other = swap(blocks[:, 1], "c")
    both = blocks[:, 0].astype(jnp.float32) + other.astype(jnp.float32)
    if middle is not None:
        both = middle(both)
    both = low(both).reshape(2, 4, 32, width)
    total = both[:, 0].astype(jnp.float32)
    for step in range(1, 4):
        total = total + ring(both[:, step], -step).astype(jnp.float32)
    return total.reshape(OWN, width)


def plane_gather(piece):
    return lax.all_to_all(jnp.broadcast_to(piece[None], (16, *piece.shape)), PLANE, 0, 0)


def plane_scatter(parts):
    return jnp.sum(lax.all_to_all(parts, PLANE, 0, 0).astype(jnp.float32), axis=0)


def all_sum(values):
    values = values + swap(values, "c")
    values = values + ring(values, 1) + ring(values, 2) + ring(values, 3)
    for axis in PLANE:
        around = [
            lax.ppermute(values, axis, [(i, (i + step) % 4) for i in range(4)])
            for step in range(1, 4)
        ]
        values = values + around[0] + around[1] + around[2]
    return values


def forward_kernel(q_ref, kv_ref, place_ref, key_ref, out_ref):
    at = place_ref[:, 0:1]
    start = place_ref[:, 1:2]

    def part(count):
        spot = key_ref[:, :count]
        allowed = (spot <= at) & (spot >= start)
        keys = kv_ref[:count, :HEAD]
        values = kv_ref[:count, HEAD:]
        lane = lax.broadcasted_iota(jnp.int32, (256, 128), 1)
        stats = jnp.zeros((256, 128), jnp.float32)
        for h in range(HEADS):
            cols = slice(h * HEAD, (h + 1) * HEAD)
            scores = times_transpose(q_ref[:, cols], keys) * 0.0625
            expos = jnp.where(allowed, jnp.exp(scores), 0.0)
            total = jnp.sum(expos, axis=-1, keepdims=True)
            out_ref[:, cols] = low(product(low(expos), values))
            high = low(total).astype(jnp.float32)
            stats = jnp.where(lane == h, high, jnp.where(lane == HEADS + h, total - high, stats))
        out_ref[:, HEADS * HEAD :] = low(stats)

    pl.when(pl.program_id(0) == 0)(lambda: part(KEYS // 2))
    pl.when(pl.program_id(0) == 1)(lambda: part(KEYS))


def attend(queries, keys_values, places, spots):
    return pl.pallas_call(
        forward_kernel,
        grid=(2,),
        in_specs=[
            pl.BlockSpec((256, HEADS * HEAD), lambda i: (i, 0)),
            pl.BlockSpec((KEYS, 2 * HEAD), lambda i: (0, 0)),
            pl.BlockSpec((256, 2), lambda i: (i, 0)),
            pl.BlockSpec((1, KEYS), lambda i: (0, 0)),
        ],
        out_specs=pl.BlockSpec((256, HEADS * HEAD + 128), lambda i: (i, 0)),
        out_shape=jax.ShapeDtypeStruct((GROUP, HEADS * HEAD + 128), jnp.bfloat16),
        compiler_params=pltpu.CompilerParams(vmem_limit_bytes=VMEM_LIMIT),
    )(queries, keys_values, places, spots)


def backward_kernel(q_ref, kv_ref, place_ref, key_ref, up_ref, stat_ref, dq_ref, dkv_ref, sum_ref):
    at = place_ref[:, 0:1]
    start = place_ref[:, 1:2]

    def part(count, first):
        spot = key_ref[:, :count]
        allowed = (spot <= at) & (spot >= start)
        keys = kv_ref[:count, :HEAD]
        values = kv_ref[:count, HEAD:]
        key_sum = jnp.zeros((count, HEAD), jnp.float32)
        value_sum = jnp.zeros((count, HEAD), jnp.float32)
        for h in range(HEADS):
            cols = slice(h * HEAD, (h + 1) * HEAD)
            query = q_ref[:, cols]
            up = up_ref[:, cols]
            scores = times_transpose(query, keys) * 0.0625
            probs = jnp.where(allowed, jnp.exp(scores), 0.0) * stat_ref[:, h : h + 1]
            probs_up = times_transpose(up, values)
            score_up = low(probs * (probs_up - stat_ref[:, HEADS + h : HEADS + h + 1]))
            dq_ref[:, cols] = low(product(score_up, keys) * 0.0625)
            key_sum = key_sum + left_product(score_up, query)
            value_sum = value_sum + left_product(low(probs), up)
        if first:
            sum_ref[:count, :HEAD] = key_sum
            sum_ref[:count, HEAD:] = value_sum
        else:
            half = KEYS // 2
            dkv_ref[:half, :HEAD] = low((sum_ref[:, :HEAD] + key_sum[:half]) * 0.0625)
            dkv_ref[:half, HEAD:] = low(sum_ref[:, HEAD:] + value_sum[:half])
            dkv_ref[half:, :HEAD] = low(key_sum[half:] * 0.0625)
            dkv_ref[half:, HEAD:] = low(value_sum[half:])

    pl.when(pl.program_id(0) == 0)(lambda: part(KEYS // 2, True))
    pl.when(pl.program_id(0) == 1)(lambda: part(KEYS, False))


def attend_back(queries, keys_values, places, spots, upstream, stats):
    return pl.pallas_call(
        backward_kernel,
        grid=(2,),
        in_specs=[
            pl.BlockSpec((256, HEADS * HEAD), lambda i: (i, 0)),
            pl.BlockSpec((KEYS, 2 * HEAD), lambda i: (0, 0)),
            pl.BlockSpec((256, 2), lambda i: (i, 0)),
            pl.BlockSpec((1, KEYS), lambda i: (0, 0)),
            pl.BlockSpec((256, HEADS * HEAD), lambda i: (i, 0)),
            pl.BlockSpec((256, 2 * HEADS), lambda i: (i, 0)),
        ],
        out_specs=(
            pl.BlockSpec((256, HEADS * HEAD), lambda i: (i, 0)),
            pl.BlockSpec((KEYS, 2 * HEAD), lambda i: (0, 0)),
        ),
        out_shape=(
            jax.ShapeDtypeStruct((GROUP, HEADS * HEAD), jnp.bfloat16),
            jax.ShapeDtypeStruct((KEYS, 2 * HEAD), jnp.bfloat16),
        ),
        scratch_shapes=[pltpu.VMEM((KEYS // 2, 2 * HEAD), jnp.float32)],
        compiler_params=pltpu.CompilerParams(vmem_limit_bytes=VMEM_LIMIT),
    )(queries, keys_values, places, spots, upstream, stats)


def per_device(
    hidden_in,
    cotangent,
    segment_ids,
    block_slot,
    w_query,
    w_key,
    w_value,
    w_out,
    w_gate,
    w_up,
    w_down,
    gain_in,
    gain_query,
    gain_key,
    gain_attn,
    gain_premlp,
    gain_mlpout,
):
    zh, at_x, at_y = lax.axis_index("zh"), lax.axis_index("x"), lax.axis_index("y")
    zl, core = lax.axis_index("zl"), lax.axis_index("c")
    shard = zl * 2 + core
    plane = at_x * 4 + at_y
    inner_low = (jnp.arange(WIDTH, dtype=jnp.int32)[:, None] == jnp.asarray(INNER, jnp.int32)[None, :])
    inner = inner_low.astype(jnp.float32)
    inner_low = inner_low.astype(jnp.bfloat16)
    exact = lax.Precision.HIGHEST

    def by_zh(first, second):
        return jnp.where(zh == 0, first, second)

    def part_of(weights):
        return (weights[:, :HIDDEN], weights[:, HIDDEN:])

    def packed(pieces):
        return jnp.concatenate(
            [jnp.pad(piece, ((0, 0), (0, WIDE - HIDDEN))) for piece in pieces], axis=1
        )

    halves = [part_of(w) for w in (w_gate, w_up, w_down.T)]
    keep = packed([by_zh(a, b) for a, b in halves])
    got = swap(packed([by_zh(b, a) for a, b in halves]), "zh")
    full = lax.all_gather(
        jnp.concatenate([by_zh(keep, got), by_zh(got, keep)], axis=0), PLANE, axis=0, tiled=True
    )
    full_two, full_down = full[:, : 2 * WIDE], full[:, 2 * WIDE :]

    both = jnp.concatenate([w_key, w_value], axis=1)
    quarter = lax.dynamic_slice_in_dim(both, shard * 128, 128, 1)
    eight = lax.all_gather(
        jnp.concatenate([w_query, quarter, w_out.T], axis=1), EIGHT, axis=0
    ).reshape(2, 4, ROWS, 640)
    eight = jnp.moveaxis(eight, 2, 1).reshape(2 * ROWS, 4, 640)

    def whole(piece):
        half = piece.shape[1] // 2
        mine = plane_gather(jnp.where(core == 0, piece[:, :half], piece[:, half:]))
        mine = mine.reshape(WIDTH, half)
        other = swap(mine, "c")
        return jnp.concatenate(
            [jnp.where(core == 0, mine, other), jnp.where(core == 0, other, mine)], axis=1
        )

    full_qkv = whole(
        jnp.concatenate(
            [eight[:, :, :256].reshape(72, 1024), eight[:, :, 256:384].reshape(72, 512)], axis=1
        )
    )
    full_out = whole(eight[:, :, 384:].reshape(72, 1024))
    full_query, full_kv = full_qkv[:, :1024], full_qkv[:, 1024:]

    lead = jnp.sum((segment_ids < 1).astype(jnp.int32))
    tail = jnp.sum((segment_ids < 2).astype(jnp.int32))

    def start_of(index):
        return jnp.where(index >= tail, tail, jnp.where(index >= lead, lead, 0))

    z = zh * 2 + zl
    step = jnp.arange(4, dtype=jnp.int32)
    from_z = (z - step) % 4
    near = jnp.where(
        from_z // 2 == 0,
        lax.dynamic_index_in_dim(block_slot, plane, 0, keepdims=False),
        lax.dynamic_index_in_dim(block_slot, 16 + plane, 0, keepdims=False),
    )
    flip = jnp.arange(2, dtype=jnp.int32)
    from_shard = (from_z % 2 * 2)[None, :] + jnp.where(flip == 0, core, 1 - core)[:, None]
    block = jnp.stack([near, 63 - near])[:, None, :]
    row = jnp.arange(32, dtype=jnp.int32)
    index = (block * 128 + from_shard[None] * 32)[..., None] + row
    index = index.reshape(GROUP)
    start = start_of(index)
    slots = lax.dynamic_slice_in_dim(block_slot, zh * 16, 16, 0)
    spots = jnp.stack([slots, 63 - slots])[:, :, None] * 128 + shard * 32 + row
    spots = spots.reshape(1, KEYS)
    places = jnp.stack([index, start], axis=1)
    freqs = THETA ** (-2.0 * jnp.arange(HEAD // 2, dtype=jnp.float32) / HEAD)
    angles = (index - start).astype(jnp.float32)[:, None] * freqs
    cosine, sine = jnp.cos(angles), jnp.sin(angles)

    def mine_of(rows):
        return rows.reshape(2, 8, 32, -1)[:, 0].reshape(OWN, -1)

    own_cosine, own_sine = mine_of(cosine), mine_of(sine)

    def take_own(rows):
        rows = lax.dynamic_index_in_dim(rows.reshape(2, 4, 32, WIDTH), shard, 1, keepdims=False)
        return product(rows.reshape(OWN, WIDTH), inner_low)

    def give_own(rows):
        rows = lax.all_gather(rows.reshape(2, 32, WIDTH), ("zl", "c"), axis=1)
        return rows.reshape(256, WIDTH)

    stream = take_own(hidden_in)
    upstream = take_own(cotangent)
    gains = product(jnp.stack([gain_in, gain_attn, gain_premlp, gain_mlpout]), inner, precision=exact)
    gain_in, gain_attn, gain_premlp, gain_mlpout = gains[0], gains[1], gains[2], gains[3]

    normed_in, scale_in = normalize(stream, gain_in)
    normed_low = low(normed_in)
    normed_all = gather_eight(normed_low)
    kv_lin = product(normed_low, full_kv)
    key_lin = kv_lin[:, :HEAD]
    key_normed, key_scale = normalize(key_lin, gain_key)
    own_kv = low(
        jnp.concatenate([turn(key_normed, own_cosine, own_sine), kv_lin[:, HEAD:]], axis=1)
    )
    keys_values = jnp.moveaxis(
        plane_gather(own_kv).reshape(16, 2, 32, 2 * HEAD), 1, 0
    ).reshape(KEYS, 2 * HEAD)
    query_lin = product(normed_all, full_query)
    heads_of = [slice(h * HEAD, (h + 1) * HEAD) for h in range(HEADS)]
    queries = low(
        jnp.concatenate(
            [turn(normalize(query_lin[:, c], gain_query)[0], cosine, sine) for c in heads_of],
            axis=1,
        )
    )
    partial = attend(queries, keys_values, places, spots)

    def keep_totals(rows):
        totals = rows[..., 1024:1028] + rows[..., 1028:1032]
        return jnp.concatenate(
            [rows[..., :1024], *split_two(totals), jnp.zeros_like(rows[..., 1032:])], axis=-1
        )

    reduced = scatter_eight(partial, keep_totals)
    total_inv = 1.0 / (reduced[:, 1024:1028] + reduced[:, 1028:1032])
    attended = jnp.concatenate(
        [reduced[:, c] * total_inv[:, h : h + 1] for h, c in enumerate(heads_of)], axis=1
    )
    heads_low = low(attended)
    attn_out = times_transpose(heads_low, full_out)
    attn_normed, attn_scale = normalize(attn_out, gain_attn)
    middle = stream + attn_normed
    mid_normed, mid_scale = normalize(middle, gain_premlp)
    mid_all = gather_eight(low(mid_normed))

    gate_up = product(mid_all, full_two)
    gate, up_proj = gate_up[:, :WIDE], gate_up[:, WIDE:]
    activated, gelu_pull = jax.vjp(lambda v: jax.nn.gelu(v, approximate=True), gate)
    hidden_low = low(activated * up_proj)
    branch = scatter_eight(low(times_transpose(hidden_low, full_down)))
    branch_normed, branch_scale = normalize(branch, gain_mlpout)
    mixed = low(middle + branch_normed)
    branch_grad, mlpout_term = normalize_back(branch, branch_scale, gain_mlpout, upstream)
    branch_all = gather_eight(low(branch_grad))
    hidden_grad = product(branch_all, full_down)
    (gate_grad,) = gelu_pull(hidden_grad * up_proj)
    two_low = jnp.concatenate([low(gate_grad), low(hidden_grad * activated)], axis=1)
    mid_grad = scatter_eight(low(times_transpose(two_low, full_two)))
    wide_grads = lax.psum_scatter(
        jnp.concatenate(
            [low(left_product(mid_all, two_low)), low(left_product(branch_all, hidden_low))], axis=1
        ),
        PLANE,
        scatter_dimension=0,
        tiled=True,
    )
    middle_back, premlp_term = normalize_back(middle, mid_scale, gain_premlp, mid_grad)
    middle_grad = upstream + middle_back
    attn_grad, attn_term = normalize_back(attn_out, attn_scale, gain_attn, middle_grad)
    attn_low = low(attn_grad)
    own_up = low(product(attn_low, full_out)).astype(jnp.float32)
    delta = jnp.concatenate(
        [jnp.sum(own_up[:, c] * attended[:, c], axis=-1, keepdims=True) for c in heads_of], axis=1
    )
    stats = jnp.concatenate([*split_two(total_inv), *split_two(delta)], axis=1)
    attn_all = gather_eight(
        jnp.concatenate([attn_low, low(jnp.pad(stats, ((0, 0), (0, 112))))], axis=1)
    )
    all_stats = attn_all[:, WIDTH:].astype(jnp.float32)
    all_stats = jnp.concatenate(
        [all_stats[:, 0:4] + all_stats[:, 4:8], all_stats[:, 8:12] + all_stats[:, 12:16]], axis=1
    )
    attn_all = attn_all[:, :WIDTH]
    heads_up = low(product(attn_all, full_out))
    query_part, kv_part = attend_back(queries, keys_values, places, spots, heads_up, all_stats)
    kv_back = plane_scatter(
        jnp.moveaxis(kv_part.reshape(2, 16, 32, 2 * HEAD), 0, 1).reshape(16, OWN, 2 * HEAD)
    )
    query_back = scatter_eight(query_part)
    key_grad, key_term = normalize_back(
        key_lin, key_scale, gain_key, turn(kv_back[:, :HEAD], own_cosine, -own_sine)
    )
    kv_low = low(jnp.concatenate([key_grad, kv_back[:, HEAD:]], axis=1))
    own_query = mine_of(query_lin)
    query_terms, query_lows = [], []
    for c in heads_of:
        lin = own_query[:, c]
        scale = lax.rsqrt(jnp.mean(lin * lin, axis=-1, keepdims=True) + EPSILON)
        grad, term = normalize_back(
            lin, scale, gain_query, turn(query_back[:, c], own_cosine, -own_sine)
        )
        query_terms.append(term)
        query_lows.append(low(grad))
    query_low = jnp.concatenate(query_lows, axis=1)
    in_grad = times_transpose(query_low, full_query) + times_transpose(kv_low, full_kv)
    stream_back, in_term = normalize_back(stream, scale_in, gain_in, in_grad)
    grad_in = middle_grad + stream_back

    def eighths(rows, width):
        return jnp.transpose(rows.reshape(OWN, 4, 2, width), (2, 1, 0, 3)).reshape(8, OWN, width)

    order = (from_z[None, :] * 2 + jnp.where(flip == 0, core, 1 - core)[:, None]).reshape(8)

    def exchange(parts):
        parts = lax.all_to_all(parts, EIGHT, 0, 0)
        parts = jnp.take(parts, order, axis=0)
        return jnp.moveaxis(parts.reshape(8, 2, 32, -1), 1, 0).reshape(GROUP, -1)

    lin_all = exchange(jnp.concatenate([eighths(query_low, 128), eighths(kv_low, 64)], axis=2))
    heads_all = exchange(eighths(heads_low, 128))
    narrow = jnp.concatenate(
        [low(left_product(normed_all, lin_all)), low(left_product(attn_all, heads_all))], axis=1
    )
    narrow = low(plane_scatter(narrow.reshape(16, 2 * ROWS, 320)))
    grads = jnp.concatenate([wide_grads, narrow], axis=1)
    keep = by_zh(grads[:ROWS], grads[ROWS:])
    got = swap(by_zh(grads[ROWS:], grads[:ROWS]), "zh")
    first, second = by_zh(keep, got), by_zh(got, keep)

    def joined(offset, width):
        return jnp.concatenate(
            [first[:, offset : offset + width], second[:, offset : offset + width]], axis=1
        )

    end = 3 * WIDE
    grad_gate = joined(0, HIDDEN).astype(jnp.float32)
    grad_up = joined(WIDE, HIDDEN).astype(jnp.float32)
    grad_down = joined(2 * WIDE, HIDDEN).astype(jnp.float32).T
    grad_query = joined(end, 128).astype(jnp.float32)
    grad_kv = lax.all_gather(joined(end + 128, 64), ("zl", "c"), axis=1).reshape(ROWS, 2 * HEAD)
    grad_kv = grad_kv.astype(jnp.float32)
    grad_out = joined(end + 192, 128).astype(jnp.float32).T

    terms = jnp.stack([jnp.sum(t, axis=0) for t in (in_term, attn_term, premlp_term, mlpout_term)])
    query_term = sum(jnp.sum(t, axis=0) for t in query_terms)
    sums = all_sum(
        jnp.concatenate([terms.reshape(-1), query_term, jnp.sum(key_term, axis=0)]).reshape(40, 128)
    ).reshape(-1)
    terms = times_transpose(sums[: 4 * WIDTH].reshape(4, WIDTH), inner, precision=exact)
    return (
        give_own(low(times_transpose(mixed, inner_low))),
        give_own(times_transpose(grad_in, inner, precision=exact)),
        grad_query,
        grad_kv[:, :HEAD],
        grad_kv[:, HEAD:],
        grad_out,
        grad_gate,
        grad_up,
        grad_down,
        terms[0],
        sums[4 * WIDTH : 4 * WIDTH + HEAD],
        sums[4 * WIDTH + HEAD :],
        terms[1],
        terms[2],
        terms[3],
    )


def solution(mesh):
    fine = Mesh(mesh.devices.reshape(2, 4, 4, 2, 2), ("zh", "x", "y", "zl", "c"))
    ctx, wt = ("zh", "x", "y"), ("zl", "c")
    rows, rows_wt, wt_rows = P(ctx, None), P(ctx, wt), P(wt, ctx)
    weights = (rows_wt, rows, rows, wt_rows, rows_wt, rows_wt, wt_rows)
    return jax.shard_map(
        per_device,
        mesh=fine,
        in_specs=(rows, rows, P(), P(), *weights, P(), P(), P(), P(), P(), P()),
        out_specs=(rows, rows, *weights, P(), P(), P(), P(), P(), P()),
        check_vma=False,
    )
```

```python
import jax
import jax.numpy as jnp
import numpy as np
from jax import lax
from jax.experimental import pallas as pl
from jax.experimental.pallas import tpu as pltpu
from jax.sharding import Mesh, PartitionSpec as P

EPSILON = 1e-06
THETA = 1000000.0
HEAD = 256
HEADS = 4
WIDTH = 1152
ROWS = 36
HIDDEN = 864
WIDE = 896
OWN = 64
GROUP = 512
KEYS = 1024
RING = ("zh", "zl")
EIGHT = ("zh", "zl", "c")
PLANE = ("x", "y")
VMEM_LIMIT = 56 * 1024 * 1024

_at = np.arange(WIDTH)
INNER = ((_at // ROWS) % 2 * 16 + (_at // ROWS) // 2) * ROWS + _at % ROWS


def normalize(values, gain):
    scale_inv = lax.rsqrt(jnp.mean(values * values, axis=-1, keepdims=True) + EPSILON)
    return (values * scale_inv * gain, scale_inv)


def normalize_back(values, scale_inv, gain, upstream):
    scaled = upstream * gain
    gain_term = upstream * values * scale_inv
    inner = jnp.mean(scaled * values, axis=-1, keepdims=True)
    return (scale_inv * scaled - values * scale_inv * scale_inv * scale_inv * inner, gain_term)


def turn(values, cosine, sine):
    half = values.shape[-1] // 2
    first = values[..., :half]
    second = values[..., half:]
    return jnp.concatenate(
        [first * cosine - second * sine, second * cosine + first * sine], axis=-1
    )


def product(left, right, **kw):
    return jnp.dot(left, right, preferred_element_type=jnp.float32, **kw)


def times_transpose(left, right, **kw):
    return lax.dot_general(
        left, right, (((1,), (1,)), ((), ())), preferred_element_type=jnp.float32, **kw
    )


def left_product(left, right):
    return lax.dot_general(
        left, right, (((0,), (0,)), ((), ())), preferred_element_type=jnp.float32
    )


def low(values):
    return values.astype(jnp.bfloat16)


def split_two(values):
    high = lax.reduce_precision(values, exponent_bits=8, mantissa_bits=7)
    return (high, values - high)


def swap(values, axis):
    return lax.ppermute(values, axis, [(0, 1), (1, 0)])


def ring(values, step):
    return lax.ppermute(values, RING, [(i, (i + step) % 4) for i in range(4)])


def call(body, outs, scratch=(), **kw):
    return pl.pallas_call(
        body,
        out_shape=tuple(jax.ShapeDtypeStruct(shape, kind) for shape, kind in outs),
        scratch_shapes=list(scratch),
        compiler_params=pltpu.CompilerParams(vmem_limit_bytes=VMEM_LIMIT),
        **kw,
    )


BF, F32 = jnp.bfloat16, jnp.float32
ANY = pl.BlockSpec(memory_space=pl.ANY)
SMEM = pl.BlockSpec(memory_space=pltpu.SMEM)
WHOLE = pl.BlockSpec(memory_space=pltpu.VMEM)


def call_after(body, outs, after, *args, scalars=0):
    after = after if isinstance(after, tuple) else (after,)
    return call(
        lambda *refs: body(*refs[len(after) :]),
        outs,
        in_specs=[ANY] * len(after) + [SMEM] * scalars + [WHOLE] * (len(args) - scalars),
    )(*after, *args)


def three_parts(values):
    high = low(values).astype(F32)
    mid = low(values - high).astype(F32)
    return jnp.concatenate([high, mid, values - high - mid], axis=0)


def gather_eight(piece):
    parts = [piece] + [ring(piece, step) for step in range(1, 4)]
    return parts + [swap(part, "c") for part in parts]


def add_split_kernel(totals, halves, a_ref, b_ref, *out_refs):
    both = a_ref[...].astype(F32) + b_ref[...].astype(F32)
    if totals:
        stats = both[:, 1024:]
        lane = lax.broadcasted_iota(jnp.int32, stats.shape, 1)
        summed = stats + pltpu.roll(stats, 128 - HEADS, 1)
        high = low(summed).astype(F32)
        rest = pltpu.roll(summed - high, HEADS, 1)
        stats = jnp.where(lane < HEADS, high, jnp.where(lane < 2 * HEADS, rest, 0.0))
        both = jnp.concatenate([both[:, :1024], stats], axis=1)
    both = low(both)
    for step in range(4):
        if halves:
            at = 32 * step
            out_refs[step][:32] = both[at : at + 32]
            out_refs[step][32:] = both[128 + at : 160 + at]
        else:
            out_refs[step][...] = both[64 * step : 64 * step + 64]


def scatter_eight(near, far, halves, totals=False):
    width = near.shape[-1]
    pieces = call(
        lambda *refs: add_split_kernel(totals, halves, *refs), [((OWN, width), BF)] * 4
    )(near, swap(far, "c"))
    return [pieces[0]] + [ring(pieces[step], -step) for step in range(1, 4)]


def summed(refs):
    total = refs[0][...].astype(F32)
    for ref in refs[1:]:
        total = total + ref[...].astype(F32)
    return total


def column_sum(term):
    return jnp.sum(term, axis=0, keepdims=True)


def prepare_kernel(own_ref, up_ref, gi_ref, ga_ref, gp_ref, gm_ref, inner_ref, x_ref, dy_ref, g_ref, n_ref):
    gains = [gi_ref[...], ga_ref[...], gp_ref[...], gm_ref[...]] * 2
    rows = [own_ref[...], up_ref[...], low(three_parts(jnp.concatenate(gains, axis=0)))]
    rows = product(jnp.concatenate(rows, axis=0), inner_ref[...])
    gains = rows[128:136] + rows[136:144] + rows[144:152]
    g_ref[...] = gains
    stream = rows[:OWN]
    x_ref[...] = stream
    dy_ref[...] = rows[OWN:128]
    n_ref[...] = low(normalize(stream, gains[0:1])[0])


def block_kernel(start, stop, z_ref, p0, p1, p2, p3, out_ref):
    pieces = (p0, p1, p2, p3)
    for z in range(4):

        def place(z=z):
            at = [pieces[(z - source) % 4][:, start:stop] for source in range(4)]
            out_ref[...] = jnp.concatenate(
                [jnp.concatenate(at[:2], axis=1), jnp.concatenate(at[2:], axis=1)], axis=0
            )

        pl.when(z_ref[0] == z)(place)


def weights_kernel(start, stop, z_ref, p0, p1, p2, p3, out_ref):
    pieces = (p0, p1, p2, p3)
    for z in range(4):

        def place(z=z):
            at = [pieces[(z - source) % 4][:, start:stop] for source in range(4)]
            block = jnp.concatenate(
                [jnp.concatenate(at[:2], axis=1), jnp.concatenate(at[2:], axis=1)], axis=0
            )
            for i in range(16):
                out_ref[i] = block

        pl.when(z_ref[0] == z)(place)


def spread_weights(start, stop, after, z, pieces):
    return call_after(
        lambda *refs: weights_kernel(start, stop, *refs),
        [((16, 72, 2 * (stop - start)), BF)],
        after,
        z.reshape(1),
        *pieces,
        scalars=1,
    )[0]


def pack_kernel(z_ref, gate_ref, up_ref, down_ref, keep_ref, give_ref):
    pad = jnp.zeros((ROWS, WIDE - HIDDEN), BF)
    for z in range(2):

        def place(z=z):
            for i, ref in enumerate((gate_ref, up_ref, down_ref)):
                rows = ref[...]
                sides = (rows[:, :HIDDEN], rows[:, HIDDEN:])
                cols = slice(i * WIDE, (i + 1) * WIDE)
                keep_ref[:, cols] = jnp.concatenate([sides[z], pad], axis=1)
                give_ref[:, cols] = jnp.concatenate([sides[1 - z], pad], axis=1)

        pl.when(z_ref[0] == z)(place)


def both_rows_kernel(z_ref, keep_ref, got_ref, out_ref):
    for z in range(2):

        def place(z=z):
            sides = (keep_ref[...], got_ref[...])
            out_ref[...] = jnp.concatenate([sides[z], sides[1 - z]], axis=0)

        pl.when(z_ref[0] == z)(place)


def rows_kernel(z_ref, got_ref, keep_ref, give_ref):
    for z in range(2):

        def place(z=z):
            grads = got_ref[...]
            sides = (grads[:ROWS], grads[ROWS:])
            keep_ref[...] = sides[z]
            give_ref[...] = sides[1 - z]

        pl.when(z_ref[0] == z)(place)


def narrow_rows_kernel(z_ref, got_ref, keep_ref, give_ref, sum_ref):
    total = jnp.sum(got_ref[...].astype(F32), axis=0)
    sum_ref[...] = total[72:88] + total[88:]
    for z in range(2):

        def place(z=z):
            sides = (low(total[:ROWS]), low(total[ROWS:72]))
            keep_ref[...] = sides[z]
            give_ref[...] = sides[1 - z]

        pl.when(z_ref[0] == z)(place)


def query_kernel(*refs):
    pieces, (w_ref, gain_ref, cos_ref, sin_ref, all_ref, q_ref, lin_ref) = refs[:8], refs[8:]
    for j in range(8):
        all_ref[32 * j : 32 * j + 32] = pieces[j][:32]
        all_ref[256 + 32 * j : 288 + 32 * j] = pieces[j][32:]
    rows = all_ref[...]
    for h in range(HEADS):
        cols = slice(h * HEAD, (h + 1) * HEAD)
        lin = product(rows, w_ref[:, cols])
        lin_ref[:32, cols] = lin[:32]
        lin_ref[32:, cols] = lin[256:288]
        q_ref[:, cols] = low(turn(normalize(lin, gain_ref[...])[0], cos_ref[...], sin_ref[...]))


def key_kernel(n_ref, w_ref, gain_ref, cos_ref, sin_ref, lin_ref, all_ref):
    lin = product(n_ref[...], w_ref[...])
    lin_ref[...] = lin[:, :HEAD]
    keys = turn(normalize(lin[:, :HEAD], gain_ref[...])[0], cos_ref[...], sin_ref[...])
    block = low(jnp.concatenate([keys, lin[:, HEAD:]], axis=1))
    for i in range(16):
        all_ref[i] = block


def plane_exchange(parts):
    return lax.all_to_all(parts, PLANE, 0, 0)


def load_keys(kv_ref, all_ref):
    for i in range(16):
        all_ref[32 * i : 32 * i + 32] = kv_ref[i, :32]
        all_ref[512 + 32 * i : 544 + 32 * i] = kv_ref[i, 32:]


def forward_kernel(q_ref, kv_ref, place_ref, key_ref, near_ref, far_ref, all_ref):
    at = place_ref[:, 0:1]
    start = place_ref[:, 1:2]
    pl.when(pl.program_id(0) == 0)(lambda: load_keys(kv_ref, all_ref))

    def part(count):
        spot = key_ref[:, :count]
        allowed = (spot <= at) & (spot >= start)
        keys = all_ref[:count, :HEAD]
        values = all_ref[:count, HEAD:]
        lane = lax.broadcasted_iota(jnp.int32, (256, 128), 1)
        stats = jnp.zeros((256, 128), F32)
        for h in range(HEADS):
            cols = slice(h * HEAD, (h + 1) * HEAD)
            scores = times_transpose(q_ref[:, cols], keys) * 0.0625
            expos = jnp.where(allowed, jnp.exp(scores), 0.0)
            total = jnp.sum(expos, axis=-1, keepdims=True)
            heads = low(product(low(expos), values))
            near_ref[:, cols] = heads[:128]
            far_ref[:, cols] = heads[128:]
            high = low(total).astype(F32)
            stats = jnp.where(lane == h, high, jnp.where(lane == HEADS + h, total - high, stats))
        near_ref[:, HEADS * HEAD :] = low(stats[:128])
        far_ref[:, HEADS * HEAD :] = low(stats[128:])

    pl.when(pl.program_id(0) == 0)(lambda: part(KEYS // 2))
    pl.when(pl.program_id(0) == 1)(lambda: part(KEYS))


def attend(queries, keys_values, places, spots):
    width = HEADS * HEAD + 128
    return call(
        forward_kernel,
        [((256, width), BF)] * 2,
        [pltpu.VMEM((KEYS, 2 * HEAD), BF)],
        grid=(2,),
        in_specs=[
            pl.BlockSpec((256, HEADS * HEAD), lambda i: (i, 0)),
            pl.BlockSpec((16, OWN, 2 * HEAD), lambda i: (0, 0, 0)),
            pl.BlockSpec((256, 2), lambda i: (i, 0)),
            pl.BlockSpec((1, KEYS), lambda i: (0, 0)),
        ],
        out_specs=(pl.BlockSpec((128, width), lambda i: (i, 0)),) * 2,
    )(queries, keys_values, places, spots)


def middle_kernel(*refs):
    pieces, (w_ref, x_ref, g_ref, att_ref, out_ref, mid_ref, n_ref, inv_ref) = refs[:4], refs[4:]
    reduced = summed(pieces)
    totals = reduced[:, 1024:] + pltpu.roll(reduced[:, 1024:], 128 - HEADS, 1)
    lane = lax.broadcasted_iota(jnp.int32, totals.shape, 1)
    inverse = 1.0 / jnp.where(lane < HEADS, totals, 1.0)
    inv_ref[...] = inverse
    attended = jnp.concatenate(
        [reduced[:, h * HEAD : (h + 1) * HEAD] * inverse[:, h : h + 1] for h in range(HEADS)], axis=1
    )
    att_ref[...] = attended
    attn_out = times_transpose(low(attended), w_ref[...])
    out_ref[...] = attn_out
    middle = x_ref[...] + normalize(attn_out, g_ref[1:2])[0]
    mid_ref[...] = middle
    n_ref[...] = low(normalize(middle, g_ref[2:3])[0])


ROOT = 0.7978845608028654


def hidden_kernel(*refs):
    pieces, (w_ref, all_ref, slope_ref, act_ref, hid_ref, near_ref, far_ref) = refs[:8], refs[8:]
    for j in range(8):
        all_ref[64 * j : 64 * j + 64] = pieces[j][...]
    for half, out_ref in ((0, near_ref), (1, far_ref)):
        own = slice(256 * half, 256 * half + 256)
        rows = all_ref[own]
        gate = product(rows, w_ref[:, :WIDE])
        up = product(rows, w_ref[:, WIDE : 2 * WIDE])
        square = gate * gate
        bend = jnp.tanh(ROOT * (gate + 0.044715 * square * gate))
        act = 0.5 * gate * (1.0 + bend)
        slope = 0.5 * (1.0 + bend) + 0.5 * gate * (1.0 - bend * bend) * (
            ROOT * (1.0 + 3.0 * 0.044715 * square)
        )
        slope_ref[own] = low(slope * up)
        act_ref[own] = low(act)
        hidden = low(act * up)
        hid_ref[own] = hidden
        out_ref[...] = low(times_transpose(hidden, w_ref[:, 2 * WIDE :]))


def turning_kernel(*refs):
    pieces, (mid_ref, dy_ref, g_ref, mixed_ref, low_ref, term_ref) = refs[:4], refs[4:]
    branch = summed(pieces)
    gain = g_ref[3:4]
    normed, scale = normalize(branch, gain)
    mixed_ref[...] = low(mid_ref[...] + normed)
    grad, term = normalize_back(branch, scale, gain, dy_ref[...])
    low_ref[...] = low(grad)
    term_ref[...] = column_sum(term)


def hidden_back_kernel(*refs):
    pieces, (w_ref, slope_ref, act_ref, all_ref, two_ref, near_ref, far_ref) = refs[:8], refs[8:]
    for j in range(8):
        all_ref[64 * j : 64 * j + 64] = pieces[j][...]
    for half, out_ref in ((0, near_ref), (1, far_ref)):
        own = slice(256 * half, 256 * half + 256)
        grad = product(all_ref[own], w_ref[:, 2 * WIDE :])
        gate = low(grad * slope_ref[own].astype(F32))
        up = low(grad * act_ref[own].astype(F32))
        two_ref[own, :WIDE] = gate
        two_ref[own, WIDE:] = up
        out_ref[...] = low(
            times_transpose(gate, w_ref[:, :WIDE]) + times_transpose(up, w_ref[:, WIDE : 2 * WIDE])
        )


def wide_kernel(after_ref, mid_ref, branch_ref, two_ref, hid_ref, out_ref):
    pl.when(pl.program_id(0) < 2)(
        lambda: out_ref.__setitem__(..., low(left_product(mid_ref[...], two_ref[...])))
    )
    pl.when(pl.program_id(0) == 2)(
        lambda: out_ref.__setitem__(..., low(left_product(branch_ref[...], hid_ref[...])))
    )


def wide_products(after, mid_all, branch_all, two_low, hidden_low):
    return call(
        wide_kernel,
        [((WIDTH, 3 * WIDE), BF)],
        grid=(3,),
        in_specs=[
            ANY,
            pl.BlockSpec((GROUP, WIDTH), lambda i: (0, 0)),
            pl.BlockSpec((GROUP, WIDTH), lambda i: (0, 0)),
            pl.BlockSpec((GROUP, WIDE), lambda i: (0, jnp.minimum(i, 1))),
            pl.BlockSpec((GROUP, WIDE), lambda i: (0, 0)),
        ],
        out_specs=(pl.BlockSpec((WIDTH, WIDE), lambda i: (0, i)),),
    )(after, mid_all, branch_all, two_low, hidden_low)[0]


def attn_turn_kernel(*refs):
    pieces = refs[:4]
    mid_ref, dy_ref, g_ref, attn_ref, att_ref, inv_ref, w_ref = refs[4:11]
    grad_ref, pack_ref, prem_ref, term_ref = refs[11:]
    middle = mid_ref[...]
    gain = g_ref[2:3]
    back, term = normalize_back(middle, normalize(middle, gain)[1], gain, summed(pieces))
    prem_ref[...] = column_sum(term)
    middle_grad = dy_ref[...] + back
    grad_ref[...] = middle_grad
    attn_out = attn_ref[...]
    gain = g_ref[1:2]
    grad, term = normalize_back(attn_out, normalize(attn_out, gain)[1], gain, middle_grad)
    term_ref[...] = column_sum(term)
    attn_low = low(grad)
    pack_ref[:, :WIDTH] = attn_low
    both = low(product(attn_low, w_ref[...])).astype(F32) * att_ref[...]
    lane = lax.broadcasted_iota(jnp.int32, (OWN, 128), 1)
    inverse = inv_ref[...]
    high = low(inverse).astype(F32)
    stats = jnp.where(lane < HEADS, high, pltpu.roll(inverse - high, HEADS, 1))
    for h in range(HEADS):
        delta = jnp.sum(both[:, h * HEAD : (h + 1) * HEAD], axis=-1, keepdims=True)
        high = low(delta).astype(F32)
        stats = jnp.where(lane == 2 * HEADS + h, high, stats)
        stats = jnp.where(lane == 3 * HEADS + h, delta - high, stats)
    pack_ref[:, WIDTH:] = low(jnp.where(lane < 4 * HEADS, stats, 0.0))


def heads_up_kernel(*refs):
    pieces, (w_ref, all_ref, up_ref, stat_ref) = refs[:8], refs[8:]
    for j in range(8):
        for half in (0, 1):
            to = slice(256 * half + 32 * j, 256 * half + 32 * j + 32)
            own = slice(32 * half, 32 * half + 32)
            all_ref[to] = pieces[j][own, :WIDTH]
            stats = pieces[j][own, WIDTH:].astype(F32)
            stat_ref[to] = stats + pltpu.roll(stats, 128 - HEADS, 1)
    up_ref[...] = low(product(all_ref[...], w_ref[...]))


def backward_kernel(
    q_ref, kv_ref, place_ref, key_ref, up_ref, stat_ref, near_ref, far_ref, dkv_ref, all_ref, sum_ref
):
    at = place_ref[:, 0:1]
    start = place_ref[:, 1:2]
    pl.when(pl.program_id(0) == 0)(lambda: load_keys(kv_ref, all_ref))

    def part(count, first):
        spot = key_ref[:, :count]
        allowed = (spot <= at) & (spot >= start)
        keys = all_ref[:count, :HEAD]
        values = all_ref[:count, HEAD:]
        key_sum = jnp.zeros((count, HEAD), F32)
        value_sum = jnp.zeros((count, HEAD), F32)
        for h in range(HEADS):
            cols = slice(h * HEAD, (h + 1) * HEAD)
            query = q_ref[:, cols]
            up = up_ref[:, cols]
            scores = times_transpose(query, keys) * 0.0625
            probs = jnp.where(allowed, jnp.exp(scores), 0.0) * stat_ref[:, h : h + 1]
            probs_up = times_transpose(up, values)
            delta = stat_ref[:, 2 * HEADS + h : 2 * HEADS + h + 1]
            score_up = low(probs * (probs_up - delta))
            grad = low(product(score_up, keys) * 0.0625)
            near_ref[:, cols] = grad[:128]
            far_ref[:, cols] = grad[128:]
            key_sum = key_sum + left_product(score_up, query)
            value_sum = value_sum + left_product(low(probs), up)
        if first:
            sum_ref[:, :HEAD] = key_sum
            sum_ref[:, HEAD:] = value_sum
        else:
            half = KEYS // 2
            sides = (
                low((sum_ref[:, :HEAD] + key_sum[:half]) * 0.0625),
                low(sum_ref[:, HEAD:] + value_sum[:half]),
                low(key_sum[half:] * 0.0625),
                low(value_sum[half:]),
            )
            for i in range(16):
                own = slice(32 * i, 32 * i + 32)
                dkv_ref[i, :32, :HEAD] = sides[0][own]
                dkv_ref[i, :32, HEAD:] = sides[1][own]
                dkv_ref[i, 32:, :HEAD] = sides[2][own]
                dkv_ref[i, 32:, HEAD:] = sides[3][own]

    pl.when(pl.program_id(0) == 0)(lambda: part(KEYS // 2, True))
    pl.when(pl.program_id(0) == 1)(lambda: part(KEYS, False))


def attend_back(queries, keys_values, places, spots, upstream, stats):
    return call(
        backward_kernel,
        [((256, HEADS * HEAD), BF)] * 2 + [((16, OWN, 2 * HEAD), BF)],
        [pltpu.VMEM((KEYS, 2 * HEAD), BF), pltpu.VMEM((KEYS // 2, 2 * HEAD), F32)],
        grid=(2,),
        in_specs=[
            pl.BlockSpec((256, HEADS * HEAD), lambda i: (i, 0)),
            pl.BlockSpec((16, OWN, 2 * HEAD), lambda i: (0, 0, 0)),
            pl.BlockSpec((256, 2), lambda i: (i, 0)),
            pl.BlockSpec((1, KEYS), lambda i: (0, 0)),
            pl.BlockSpec((256, HEADS * HEAD), lambda i: (i, 0)),
            pl.BlockSpec((256, 128), lambda i: (i, 0)),
        ],
        out_specs=(
            pl.BlockSpec((128, HEADS * HEAD), lambda i: (i, 0)),
            pl.BlockSpec((128, HEADS * HEAD), lambda i: (i, 0)),
            pl.BlockSpec((16, OWN, 2 * HEAD), lambda i: (0, 0, 0)),
        ),
    )(queries, keys_values, places, spots, upstream, stats)


def lin_kernel(*refs):
    pieces = refs[:4]
    kv_ref, qlin_ref, klin_ref, cos_ref, sin_ref, gq_ref, gk_ref, att_ref = refs[4:12]
    out_ref, ql_ref, kl_ref, term_ref = refs[12:]
    kv_back = jnp.sum(kv_ref[...].astype(F32), axis=0)
    back = summed(pieces)
    cosine, sine = cos_ref[...], -sin_ref[...]
    key_lin = klin_ref[...]
    gain = gk_ref[...]
    grad, term = normalize_back(
        key_lin, normalize(key_lin, gain)[1], gain, turn(kv_back[:, :HEAD], cosine, sine)
    )
    term_ref[:, HEAD:] = column_sum(term)
    kv_low = low(jnp.concatenate([grad, kv_back[:, HEAD:]], axis=1))
    kl_ref[...] = kv_low
    gain = gq_ref[...]
    total = jnp.zeros((1, HEAD), F32)
    for h in range(HEADS):
        cols = slice(h * HEAD, (h + 1) * HEAD)
        lin = qlin_ref[:, cols]
        grad, term = normalize_back(
            lin, normalize(lin, gain)[1], gain, turn(back[:, cols], cosine, sine)
        )
        total = total + column_sum(term)
        query_low = low(grad)
        ql_ref[:, cols] = query_low
        heads = low(att_ref[:, cols])
        for zh in range(2):
            at = slice(zh * 128, zh * 128 + 128)
            out_ref[zh * 4 + h, :, :128] = query_low[:, at]
            out_ref[zh * 4 + h, :, 128:256] = heads[:, at]
            out_ref[zh * 4 + h, :, 256:] = kv_low[:, h * 128 + zh * 64 : h * 128 + zh * 64 + 64]
    term_ref[:, :HEAD] = total


def input_kernel(
    ql_ref, kl_ref, wq_ref, wkv_ref, x_ref, g_ref, mg_ref, t1, t2, t3, back_ref, out_ref, term_ref
):
    grad = times_transpose(ql_ref[...], wq_ref[...]) + times_transpose(kl_ref[...], wkv_ref[...])
    stream = x_ref[...]
    gain = g_ref[0:1]
    back, term = normalize_back(stream, normalize(stream, gain)[1], gain, grad)
    out_ref[...] = low(mg_ref[...] + back)
    terms = jnp.concatenate([column_sum(term), t1[...], t2[...], t3[...]] * 2, axis=0)
    rows = product(low(three_parts(terms)), back_ref[...])
    term_ref[...] = rows[:8] + rows[8:16] + rows[16:24]


def natural_kernel(rows_ref, back_ref, out_ref):
    out_ref[...] = low(product(rows_ref[...], back_ref[...]))


def wide_out_kernel(z_ref, keep_ref, got_ref, gate_ref, up_ref, down_ref):
    for z in range(2):

        def place(z=z):
            pair = (keep_ref, got_ref) if z == 0 else (got_ref, keep_ref)
            for i, ref in enumerate((gate_ref, up_ref, down_ref)):
                cols = slice(i * WIDE, i * WIDE + HIDDEN)
                ref[...] = jnp.concatenate([half[:, cols].astype(F32) for half in pair], axis=1)

        pl.when(z_ref[0] == z)(place)


def narrow_kernel(after_ref, order_ref, lin_ref, normed_ref, attn_ref, gain_ref, out_ref, all_ref):
    for j in range(8):
        source = order_ref[j]
        all_ref[32 * j : 32 * j + 32] = lin_ref[source, :32]
        all_ref[256 + 32 * j : 288 + 32 * j] = lin_ref[source, 32:]
    normed = normed_ref[...]
    query = low(left_product(normed, all_ref[:, :128]))
    heads = low(left_product(attn_ref[...], all_ref[:, 128:256]))
    keys = low(left_product(normed, all_ref[:, 256:]))
    for i in range(16):
        own = slice(72 * i, 72 * i + 72)
        out_ref[i, :72, :128] = query[own]
        out_ref[i, :72, 128:256] = heads[own]
        out_ref[i, :72, 256:] = keys[own]
        out_ref[i, 72:, :] = gain_ref[...]


def per_device(
    hidden_in,
    cotangent,
    segment_ids,
    block_slot,
    w_query,
    w_key,
    w_value,
    w_out,
    w_gate,
    w_up,
    w_down,
    gain_in,
    gain_query,
    gain_key,
    gain_attn,
    gain_premlp,
    gain_mlpout,
):
    zh, at_x, at_y = lax.axis_index("zh"), lax.axis_index("x"), lax.axis_index("y")
    zl, core = lax.axis_index("zl"), lax.axis_index("c")
    shard = zl * 2 + core
    plane = at_x * 4 + at_y
    z = zh * 2 + zl
    place = jnp.asarray(INNER, jnp.int32)
    outer = low(place[:, None] == jnp.arange(WIDTH, dtype=jnp.int32)[None, :])
    inner = low(jnp.arange(WIDTH, dtype=jnp.int32)[:, None] == place[None, :])

    def by_zh(first, second):
        return jnp.where(zh == 0, first, second)

    both = jnp.concatenate([w_key, w_value], axis=1)
    quarter = lax.dynamic_slice_in_dim(both, shard * 128, 128, 1)
    pack = jnp.concatenate([w_query, quarter, w_out.T], axis=1)
    ring_pieces = [pack] + [ring(pack, step) for step in range(1, 4)]

    def four_heads(mine):
        other = swap(mine, "c")
        half = mine.shape[1] // 2
        first, second = jnp.where(core == 0, mine, other), jnp.where(core == 0, other, mine)
        return jnp.concatenate(
            [first[:, :half], second[:, :half], first[:, half:], second[:, half:]], axis=1
        )

    def whole(spread):
        return four_heads(spread.reshape(WIDTH, -1))

    spread_kv = spread_weights(256, 384, ring_pieces[3], z, ring_pieces)
    (out_block,) = call_after(
        lambda *refs: block_kernel(384, 640, *refs),
        [((72, 512), BF)],
        spread_kv,
        z.reshape(1),
        *ring_pieces,
        scalars=1,
    )
    full_out = lax.all_gather(four_heads(out_block), PLANE, axis=0, tiled=True)
    got_kv = plane_exchange(spread_kv)
    full_kv = whole(got_kv)

    lead = jnp.sum((segment_ids < 1).astype(jnp.int32))
    tail = jnp.sum((segment_ids < 2).astype(jnp.int32))

    def start_of(index):
        return jnp.where(index >= tail, tail, jnp.where(index >= lead, lead, 0))

    step = jnp.arange(4, dtype=jnp.int32)
    from_z = (z - step) % 4
    near = jnp.where(
        from_z // 2 == 0,
        lax.dynamic_index_in_dim(block_slot, plane, 0, keepdims=False),
        lax.dynamic_index_in_dim(block_slot, 16 + plane, 0, keepdims=False),
    )
    flip = jnp.arange(2, dtype=jnp.int32)
    from_shard = (from_z % 2 * 2)[None, :] + jnp.where(flip == 0, core, 1 - core)[:, None]
    block = jnp.stack([near, 63 - near])[:, None, :]
    row = jnp.arange(32, dtype=jnp.int32)
    index = (block * 128 + from_shard[None] * 32)[..., None] + row
    index = index.reshape(GROUP)
    start = start_of(index)
    slots = lax.dynamic_slice_in_dim(block_slot, zh * 16, 16, 0)
    spots = jnp.stack([slots, 63 - slots])[:, :, None] * 128 + shard * 32 + row
    spots = spots.reshape(1, KEYS)
    places = jnp.stack([index, start], axis=1)
    freqs = THETA ** (-2.0 * jnp.arange(HEAD // 2, dtype=jnp.float32) / HEAD)
    angles = (index - start).astype(jnp.float32)[:, None] * freqs
    cosine, sine = jnp.cos(angles), jnp.sin(angles)

    def mine_of(rows):
        return rows.reshape(2, 8, 32, -1)[:, 0].reshape(OWN, -1)

    own_cosine, own_sine = mine_of(cosine), mine_of(sine)

    own_cosine, own_sine = mine_of(cosine), mine_of(sine)

    def four_rows(rows):
        flipped = swap(rows, "zl")
        mine = jnp.stack(
            [jnp.where(zl == 0, rows, flipped), jnp.where(zl == 0, flipped, rows)]
        )
        return mine, swap(mine, "c")

    def ordered(mine, other):
        rows = jnp.stack(
            [jnp.where(core == 0, mine, other), jnp.where(core == 0, other, mine)], axis=1
        )
        return jnp.moveaxis(rows.reshape(4, 2, 32, WIDTH), 1, 0).reshape(256, WIDTH)

    def take_own(rows):
        rows = lax.dynamic_index_in_dim(rows.reshape(2, 4, 32, WIDTH), shard, 1, keepdims=False)
        return rows.reshape(OWN, WIDTH)

    one = (1, WIDTH)
    stream, upstream, gains, normed_low = call_after(
        prepare_kernel,
        [((OWN, WIDTH), F32), ((OWN, WIDTH), F32), ((8, WIDTH), F32), ((OWN, WIDTH), BF)],
        spread_kv,
        take_own(hidden_in),
        take_own(cotangent),
        *[g.reshape(one) for g in (gain_in, gain_attn, gain_premlp, gain_mlpout)],
        inner,
    )
    gain_query, gain_key = gain_query.reshape(1, HEAD), gain_key.reshape(1, HEAD)
    got_query = plane_exchange(spread_weights(0, 256, (got_kv, normed_low), z, ring_pieces))
    full_query = whole(got_query)
    key_lin, spread_keys = call(key_kernel, [((OWN, HEAD), F32), ((16, OWN, 2 * HEAD), BF)])(
        normed_low, full_kv, gain_key,
        own_cosine,
        own_sine,
    )
    keys_values = plane_exchange(spread_keys)
    normed_pieces = gather_eight(normed_low)

    keep, give = call_after(
        pack_kernel,
        [((ROWS, 3 * WIDE), BF)] * 2,
        (spread_keys, *normed_pieces[5:]),
        zh.reshape(1),
        w_gate,
        w_up,
        w_down.T,
        scalars=1,
    )
    full = lax.all_gather(
        call_after(
            both_rows_kernel,
            [((72, 3 * WIDE), BF)],
            (got_query, full_out),
            zh.reshape(1),
            keep,
            swap(give, "zh"),
            scalars=1,
        )[0],
        PLANE,
        axis=0,
        tiled=True,
    )

    normed_all, queries, query_lin = call(
        query_kernel,
        [((GROUP, WIDTH), BF), ((GROUP, HEADS * HEAD), BF), ((OWN, HEADS * HEAD), F32)],
    )(*normed_pieces, full_query, gain_query, cosine, sine)
    near, far = attend(queries, keys_values, places, spots)
    parts = scatter_eight(near, far, True, True)
    attended, attn_out, middle, mid_low, total_inv = call(
        middle_kernel,
        [
            ((OWN, HEADS * HEAD), F32),
            ((OWN, WIDTH), F32),
            ((OWN, WIDTH), F32),
            ((OWN, WIDTH), BF),
            ((OWN, 128), F32),
        ],
    )(*parts, full_out, stream, gains)

    mid_all, slope, act, hidden_low, near, far = call(
        hidden_kernel,
        [((GROUP, WIDTH), BF)] + [((GROUP, WIDE), BF)] * 3 + [((256, WIDTH), BF)] * 2,
    )(*gather_eight(mid_low), full)
    mixed, branch_low, mlpout_term = call(
        turning_kernel, [((OWN, WIDTH), BF), ((OWN, WIDTH), BF), (one, F32)]
    )(*scatter_eight(near, far, False), middle, upstream, gains)
    mixed_rows = four_rows(call(natural_kernel, [((OWN, WIDTH), BF)])(mixed, outer)[0])
    branch_all, two_low, near, far = call(
        hidden_back_kernel,
        [((GROUP, WIDTH), BF), ((GROUP, 2 * WIDE), BF)] + [((256, WIDTH), BF)] * 2,
    )(*gather_eight(branch_low), full, slope, act)
    parts = scatter_eight(near, far, False)
    wide_parts = wide_products(parts[0], mid_all, branch_all, two_low, hidden_low)
    wide = lax.psum_scatter(
        wide_parts,
        PLANE,
        scatter_dimension=0,
        tiled=True,
    )
    middle_grad, attn_pack, premlp_term, attn_term = call_after(
        attn_turn_kernel,
        [((OWN, WIDTH), F32), ((OWN, WIDTH + 128), BF), (one, F32), (one, F32)],
        wide_parts,
        *parts,
        middle,
        upstream,
        gains,
        attn_out,
        attended,
        total_inv,
        full_out,
    )
    attn_all, heads_up, stats = call_after(
        heads_up_kernel,
        [((GROUP, WIDTH), BF), ((GROUP, HEADS * HEAD), BF), ((GROUP, 128), F32)],
        mixed_rows[1],
        *gather_eight(attn_pack),
        full_out,
    )
    near, far, kv_part = attend_back(queries, keys_values, places, spots, heads_up, stats)
    lin_parts, query_low, kv_low, head_terms = call(
        lin_kernel,
        [
            ((8, OWN, 320), BF),
            ((OWN, HEADS * HEAD), BF),
            ((OWN, 2 * HEAD), BF),
            ((1, 2 * HEAD), F32),
        ],
    )(
        *scatter_eight(near, far, True),
        plane_exchange(kv_part),
        query_lin,
        key_lin,
        own_cosine,
        own_sine,
        gain_query,
        gain_key,
        attended,
    )
    grad_own, terms = call(input_kernel, [((OWN, WIDTH), BF), ((8, WIDTH), F32)])(
        query_low,
        kv_low,
        full_query,
        full_kv,
        stream,
        gains,
        middle_grad,
        attn_term,
        premlp_term,
        mlpout_term,
        outer,
    )

    def by_rows(keep, give):
        got = swap(give, "zh")
        return by_zh(keep, got), by_zh(got, keep)

    order = (from_z[None, :] * 2 + jnp.where(flip == 0, core, 1 - core)[:, None]).reshape(8)
    sums = jnp.concatenate([terms[:4].reshape(-1), head_terms.reshape(-1)]).reshape(16, 320)
    keep_wide, give_wide = call(
        rows_kernel, [((ROWS, 3 * WIDE), BF)] * 2, in_specs=[SMEM, WHOLE]
    )(zh.reshape(1), wide)
    got_wide = swap(give_wide, "zh")
    (narrow,) = call(
        narrow_kernel,
        [((16, 104, 320), BF)],
        [pltpu.VMEM((GROUP, 320), BF)],
        in_specs=[ANY, SMEM] + [WHOLE] * 4,
    )(
        got_wide,
        order,
        lax.all_to_all(lin_parts, EIGHT, 0, 0),
        normed_all,
        attn_all,
        low(jnp.concatenate(split_two(sums), axis=0)),
    )
    (grad_own,) = call_after(natural_kernel, [((OWN, WIDTH), BF)], narrow, grad_own, outer)
    grad_gate, grad_up, grad_down = call_after(
        wide_out_kernel,
        [((ROWS, 2 * HIDDEN), F32)] * 3,
        narrow,
        zh.reshape(1),
        keep_wide,
        got_wide,
        scalars=1,
    )
    keep, give, sums = call_after(
        narrow_rows_kernel,
        [((ROWS, 320), BF)] * 2 + [((16, 320), F32)],
        (grad_gate, grad_own),
        zh.reshape(1),
        plane_exchange(narrow),
        scalars=1,
    )
    narrow_pair = by_rows(keep, give)
    sums = sums + swap(sums, "c")
    sums = sums + ring(sums, 1) + ring(sums, 2) + ring(sums, 3)
    sums = sums.reshape(-1)

    def joined(pair, offset, width):
        return jnp.concatenate(
            [half[:, offset : offset + width] for half in pair], axis=1
        ).astype(F32)

    pair = narrow_pair
    grad_query = joined(pair, 0, 128)
    grad_out = joined(pair, 128, 128).T
    grad_kv = lax.all_gather(low(joined(pair, 256, 64)), ("zl", "c"), axis=1)
    grad_kv = grad_kv.reshape(ROWS, 2 * HEAD).astype(F32)

    rows = ordered(*four_rows(grad_own))
    return (
        ordered(*mixed_rows),
        rows.astype(F32),
        grad_query,
        grad_kv[:, :HEAD],
        grad_kv[:, HEAD:],
        grad_out,
        grad_gate,
        grad_up,
        grad_down.T,
        sums[:WIDTH],
        sums[4 * WIDTH : 4 * WIDTH + HEAD],
        sums[4 * WIDTH + HEAD :],
        sums[WIDTH : 2 * WIDTH],
        sums[2 * WIDTH : 3 * WIDTH],
        sums[3 * WIDTH : 4 * WIDTH],
    )


def solution(mesh):
    fine = Mesh(mesh.devices.reshape(2, 4, 4, 2, 2), ("zh", "x", "y", "zl", "c"))
    ctx, wt = ("zh", "x", "y"), ("zl", "c")
    rows, rows_wt, wt_rows = P(ctx, None), P(ctx, wt), P(wt, ctx)
    weights = (rows_wt, rows, rows, wt_rows, rows_wt, rows_wt, wt_rows)
    return jax.shard_map(
        per_device,
        mesh=fine,
        in_specs=(rows, rows, P(), P(), *weights, P(), P(), P(), P(), P(), P()),
        out_specs=(rows, rows, *weights, P(), P(), P(), P(), P(), P()),
        check_vma=False,
    )
```

```python
import jax
import jax.numpy as jnp
import numpy as np
from jax import lax
from jax.experimental import pallas as pl
from jax.experimental.pallas import tpu as pltpu
from jax.sharding import Mesh, PartitionSpec as P

EPSILON = 1e-06
THETA = 1000000.0
HEAD = 256
HEADS = 4
WIDTH = 1152
ROWS = 36
HIDDEN = 864
WIDE = 896
OWN = 64
GROUP = 512
KEYS = 1024
RING = ("zh", "zl")
EIGHT = ("zh", "zl", "c")
PLANE = ("x", "y")
VMEM_LIMIT = 56 * 1024 * 1024

_at = np.arange(WIDTH)
INNER = ((_at // ROWS) % 2 * 16 + (_at // ROWS) // 2) * ROWS + _at % ROWS


def normalize(values, gain):
    scale_inv = lax.rsqrt(jnp.mean(values * values, axis=-1, keepdims=True) + EPSILON)
    return (values * scale_inv * gain, scale_inv)


def normalize_back(values, scale_inv, gain, upstream):
    scaled = upstream * gain
    gain_term = upstream * values * scale_inv
    inner = jnp.mean(scaled * values, axis=-1, keepdims=True)
    return (scale_inv * scaled - values * scale_inv * scale_inv * scale_inv * inner, gain_term)


def turn(values, cosine, sine):
    half = values.shape[-1] // 2
    first = values[..., :half]
    second = values[..., half:]
    return jnp.concatenate(
        [first * cosine - second * sine, second * cosine + first * sine], axis=-1
    )


def product(left, right, **kw):
    return jnp.dot(left, right, preferred_element_type=jnp.float32, **kw)


def times_transpose(left, right, **kw):
    return lax.dot_general(
        left, right, (((1,), (1,)), ((), ())), preferred_element_type=jnp.float32, **kw
    )


def left_product(left, right):
    return lax.dot_general(
        left, right, (((0,), (0,)), ((), ())), preferred_element_type=jnp.float32
    )


def low(values):
    return values.astype(jnp.bfloat16)


def split_two(values):
    high = lax.reduce_precision(values, exponent_bits=8, mantissa_bits=7)
    return (high, values - high)


def swap(values, axis):
    return lax.ppermute(values, axis, [(0, 1), (1, 0)])


def ring(values, step):
    return lax.ppermute(values, RING, [(i, (i + step) % 4) for i in range(4)])


def call(body, outs, scratch=(), **kw):
    return pl.pallas_call(
        body,
        out_shape=tuple(jax.ShapeDtypeStruct(shape, kind) for shape, kind in outs),
        scratch_shapes=list(scratch),
        compiler_params=pltpu.CompilerParams(vmem_limit_bytes=VMEM_LIMIT),
        **kw,
    )


BF, F32 = jnp.bfloat16, jnp.float32
ANY = pl.BlockSpec(memory_space=pl.ANY)
SMEM = pl.BlockSpec(memory_space=pltpu.SMEM)
WHOLE = pl.BlockSpec(memory_space=pltpu.VMEM)


def call_after(body, outs, after, *args, scalars=0):
    after = after if isinstance(after, tuple) else (after,)
    return call(
        lambda *refs: body(*refs[len(after) :]),
        outs,
        in_specs=[ANY] * len(after) + [SMEM] * scalars + [WHOLE] * (len(args) - scalars),
    )(*after, *args)


def three_parts(values):
    high = low(values).astype(F32)
    mid = low(values - high).astype(F32)
    return jnp.concatenate([high, mid, values - high - mid], axis=0)


def gather_eight(piece):
    parts = [piece] + [ring(piece, step) for step in range(1, 4)]
    return parts + [swap(part, "c") for part in parts]


def add_split_kernel(totals, halves, a_ref, b_ref, *out_refs):
    both = a_ref[...].astype(F32) + b_ref[...].astype(F32)
    if totals:
        stats = both[:, 1024:]
        lane = lax.broadcasted_iota(jnp.int32, stats.shape, 1)
        summed = stats + pltpu.roll(stats, 128 - HEADS, 1)
        high = low(summed).astype(F32)
        rest = pltpu.roll(summed - high, HEADS, 1)
        stats = jnp.where(lane < HEADS, high, jnp.where(lane < 2 * HEADS, rest, 0.0))
        both = jnp.concatenate([both[:, :1024], stats], axis=1)
    both = low(both)
    for step in range(4):
        if halves:
            at = 32 * step
            out_refs[step][:32] = both[at : at + 32]
            out_refs[step][32:] = both[128 + at : 160 + at]
        else:
            out_refs[step][...] = both[64 * step : 64 * step + 64]


def scatter_eight(near, far, halves, totals=False):
    width = near.shape[-1]
    pieces = call(
        lambda *refs: add_split_kernel(totals, halves, *refs), [((OWN, width), BF)] * 4
    )(near, swap(far, "c"))
    return [pieces[0]] + [ring(pieces[step], -step) for step in range(1, 4)]


def summed(refs):
    total = refs[0][...].astype(F32)
    for ref in refs[1:]:
        total = total + ref[...].astype(F32)
    return total


def column_sum(term):
    return jnp.sum(term, axis=0, keepdims=True)


def prepare_kernel(own_ref, up_ref, gi_ref, ga_ref, gp_ref, gm_ref, inner_ref, x_ref, dy_ref, g_ref, n_ref):
    gains = [gi_ref[...], ga_ref[...], gp_ref[...], gm_ref[...]] * 2
    rows = [own_ref[...], up_ref[...], low(three_parts(jnp.concatenate(gains, axis=0)))]
    rows = product(jnp.concatenate(rows, axis=0), inner_ref[...])
    gains = rows[128:136] + rows[136:144] + rows[144:152]
    g_ref[...] = gains
    stream = rows[:OWN]
    x_ref[...] = stream
    dy_ref[...] = rows[OWN:128]
    n_ref[...] = low(normalize(stream, gains[0:1])[0])


def block_kernel(start, stop, z_ref, p0, p1, p2, p3, out_ref):
    pieces = (p0, p1, p2, p3)
    for z in range(4):

        def place(z=z):
            at = [pieces[(z - source) % 4][:, start:stop] for source in range(4)]
            out_ref[...] = jnp.concatenate(
                [jnp.concatenate(at[:2], axis=1), jnp.concatenate(at[2:], axis=1)], axis=0
            )

        pl.when(z_ref[0] == z)(place)


def weights_kernel(start, stop, z_ref, p0, p1, p2, p3, out_ref):
    pieces = (p0, p1, p2, p3)
    for z in range(4):

        def place(z=z):
            at = [pieces[(z - source) % 4][:, start:stop] for source in range(4)]
            block = jnp.concatenate(
                [jnp.concatenate(at[:2], axis=1), jnp.concatenate(at[2:], axis=1)], axis=0
            )
            for i in range(16):
                out_ref[i] = block

        pl.when(z_ref[0] == z)(place)


def spread_weights(start, stop, after, z, pieces):
    return call_after(
        lambda *refs: weights_kernel(start, stop, *refs),
        [((16, 72, 2 * (stop - start)), BF)],
        after,
        z.reshape(1),
        *pieces,
        scalars=1,
    )[0]


def pack_kernel(z_ref, gate_ref, up_ref, down_ref, keep_ref, give_ref):
    pad = jnp.zeros((ROWS, WIDE - HIDDEN), BF)
    for z in range(2):

        def place(z=z):
            for i, ref in enumerate((gate_ref, up_ref, down_ref)):
                rows = ref[...]
                sides = (rows[:, :HIDDEN], rows[:, HIDDEN:])
                cols = slice(i * WIDE, (i + 1) * WIDE)
                keep_ref[:, cols] = jnp.concatenate([sides[z], pad], axis=1)
                give_ref[:, cols] = jnp.concatenate([sides[1 - z], pad], axis=1)

        pl.when(z_ref[0] == z)(place)


def both_rows_kernel(z_ref, keep_ref, got_ref, out_ref):
    for z in range(2):

        def place(z=z):
            sides = (keep_ref[...], got_ref[...])
            out_ref[...] = jnp.concatenate([sides[z], sides[1 - z]], axis=0)

        pl.when(z_ref[0] == z)(place)


def rows_kernel(z_ref, got_ref, keep_ref, give_ref):
    for z in range(2):

        def place(z=z):
            grads = got_ref[...]
            sides = (grads[:ROWS], grads[ROWS:])
            keep_ref[...] = sides[z]
            give_ref[...] = sides[1 - z]

        pl.when(z_ref[0] == z)(place)


def narrow_rows_kernel(z_ref, got_ref, keep_ref, give_ref, sum_ref):
    total = jnp.sum(got_ref[...].astype(F32), axis=0)
    sum_ref[...] = total[72:88] + total[88:]
    for z in range(2):

        def place(z=z):
            sides = (low(total[:ROWS]), low(total[ROWS:72]))
            keep_ref[...] = sides[z]
            give_ref[...] = sides[1 - z]

        pl.when(z_ref[0] == z)(place)


def query_kernel(*refs):
    pieces, (w_ref, gain_ref, cos_ref, sin_ref, all_ref, q_ref, lin_ref) = refs[:8], refs[8:]
    for j in range(8):
        all_ref[32 * j : 32 * j + 32] = pieces[j][:32]
        all_ref[256 + 32 * j : 288 + 32 * j] = pieces[j][32:]
    rows = all_ref[...]
    for h in range(HEADS):
        cols = slice(h * HEAD, (h + 1) * HEAD)
        lin = product(rows, w_ref[:, cols])
        lin_ref[:32, cols] = lin[:32]
        lin_ref[32:, cols] = lin[256:288]
        q_ref[:, cols] = low(turn(normalize(lin, gain_ref[...])[0], cos_ref[...], sin_ref[...]))


def key_kernel(n_ref, w_ref, gain_ref, cos_ref, sin_ref, lin_ref, all_ref):
    lin = product(n_ref[...], w_ref[...])
    lin_ref[...] = lin[:, :HEAD]
    keys = turn(normalize(lin[:, :HEAD], gain_ref[...])[0], cos_ref[...], sin_ref[...])
    block = low(jnp.concatenate([keys, lin[:, HEAD:]], axis=1))
    for i in range(16):
        all_ref[i] = block


def plane_exchange(parts):
    return lax.all_to_all(parts, PLANE, 0, 0)


def load_keys(kv_ref, all_ref):
    for i in range(16):
        all_ref[32 * i : 32 * i + 32] = kv_ref[i, :32]
        all_ref[512 + 32 * i : 544 + 32 * i] = kv_ref[i, 32:]


def forward_kernel(q_ref, kv_ref, place_ref, key_ref, near_ref, far_ref, all_ref):
    at = place_ref[:, 0:1]
    start = place_ref[:, 1:2]
    pl.when(pl.program_id(0) == 0)(lambda: load_keys(kv_ref, all_ref))

    def part(count):
        spot = key_ref[:, :count]
        allowed = (spot <= at) & (spot >= start)
        keys = all_ref[:count, :HEAD]
        values = all_ref[:count, HEAD:]
        lane = lax.broadcasted_iota(jnp.int32, (256, 128), 1)
        stats = jnp.zeros((256, 128), F32)
        for h in range(HEADS):
            cols = slice(h * HEAD, (h + 1) * HEAD)
            scores = times_transpose(q_ref[:, cols], keys) * 0.0625
            expos = jnp.where(allowed, jnp.exp(scores), 0.0)
            total = jnp.sum(expos, axis=-1, keepdims=True)
            heads = low(product(low(expos), values))
            near_ref[:, cols] = heads[:128]
            far_ref[:, cols] = heads[128:]
            high = low(total).astype(F32)
            stats = jnp.where(lane == h, high, jnp.where(lane == HEADS + h, total - high, stats))
        near_ref[:, HEADS * HEAD :] = low(stats[:128])
        far_ref[:, HEADS * HEAD :] = low(stats[128:])

    pl.when(pl.program_id(0) == 0)(lambda: part(KEYS // 2))
    pl.when(pl.program_id(0) == 1)(lambda: part(KEYS))


def attend(queries, keys_values, places, spots):
    width = HEADS * HEAD + 128
    return call(
        forward_kernel,
        [((256, width), BF)] * 2,
        [pltpu.VMEM((KEYS, 2 * HEAD), BF)],
        grid=(2,),
        in_specs=[
            pl.BlockSpec((256, HEADS * HEAD), lambda i: (i, 0)),
            pl.BlockSpec((16, OWN, 2 * HEAD), lambda i: (0, 0, 0)),
            pl.BlockSpec((256, 2), lambda i: (i, 0)),
            pl.BlockSpec((1, KEYS), lambda i: (0, 0)),
        ],
        out_specs=(pl.BlockSpec((128, width), lambda i: (i, 0)),) * 2,
    )(queries, keys_values, places, spots)


def middle_kernel(*refs):
    pieces, (w_ref, x_ref, g_ref, att_ref, out_ref, mid_ref, n_ref, inv_ref) = refs[:4], refs[4:]
    reduced = summed(pieces)
    totals = reduced[:, 1024:] + pltpu.roll(reduced[:, 1024:], 128 - HEADS, 1)
    lane = lax.broadcasted_iota(jnp.int32, totals.shape, 1)
    inverse = 1.0 / jnp.where(lane < HEADS, totals, 1.0)
    inv_ref[...] = inverse
    attended = jnp.concatenate(
        [reduced[:, h * HEAD : (h + 1) * HEAD] * inverse[:, h : h + 1] for h in range(HEADS)], axis=1
    )
    att_ref[...] = attended
    attn_out = times_transpose(low(attended), w_ref[...])
    out_ref[...] = attn_out
    middle = x_ref[...] + normalize(attn_out, g_ref[1:2])[0]
    mid_ref[...] = middle
    n_ref[...] = low(normalize(middle, g_ref[2:3])[0])


ROOT = 0.7978845608028654


def hidden_kernel(*refs):
    pieces, (w_ref, all_ref, slope_ref, act_ref, hid_ref, near_ref, far_ref) = refs[:8], refs[8:]
    for j in range(8):
        all_ref[64 * j : 64 * j + 64] = pieces[j][...]
    for half, out_ref in ((0, near_ref), (1, far_ref)):
        own = slice(256 * half, 256 * half + 256)
        rows = all_ref[own]
        gate = product(rows, w_ref[:, :WIDE])
        up = product(rows, w_ref[:, WIDE : 2 * WIDE])
        square = gate * gate
        bend = jnp.tanh(ROOT * (gate + 0.044715 * square * gate))
        act = 0.5 * gate * (1.0 + bend)
        slope = 0.5 * (1.0 + bend) + 0.5 * gate * (1.0 - bend * bend) * (
            ROOT * (1.0 + 3.0 * 0.044715 * square)
        )
        slope_ref[own] = low(slope * up)
        act_ref[own] = low(act)
        hidden = low(act * up)
        hid_ref[own] = hidden
        out_ref[...] = low(times_transpose(hidden, w_ref[:, 2 * WIDE :]))


def turning_kernel(*refs):
    pieces, (mid_ref, dy_ref, g_ref, mixed_ref, low_ref, term_ref) = refs[:4], refs[4:]
    branch = summed(pieces)
    gain = g_ref[3:4]
    normed, scale = normalize(branch, gain)
    mixed_ref[...] = low(mid_ref[...] + normed)
    grad, term = normalize_back(branch, scale, gain, dy_ref[...])
    low_ref[...] = low(grad)
    term_ref[...] = column_sum(term)


def hidden_back_kernel(*refs):
    pieces, (w_ref, slope_ref, act_ref, all_ref, two_ref, near_ref, far_ref) = refs[:8], refs[8:]
    for j in range(8):
        all_ref[64 * j : 64 * j + 64] = pieces[j][...]
    for half, out_ref in ((0, near_ref), (1, far_ref)):
        own = slice(256 * half, 256 * half + 256)
        grad = product(all_ref[own], w_ref[:, 2 * WIDE :])
        gate = low(grad * slope_ref[own].astype(F32))
        up = low(grad * act_ref[own].astype(F32))
        two_ref[own, :WIDE] = gate
        two_ref[own, WIDE:] = up
        out_ref[...] = low(
            times_transpose(gate, w_ref[:, :WIDE]) + times_transpose(up, w_ref[:, WIDE : 2 * WIDE])
        )


def wide_kernel(after_ref, mid_ref, branch_ref, two_ref, hid_ref, out_ref):
    pl.when(pl.program_id(0) < 2)(
        lambda: out_ref.__setitem__(..., low(left_product(mid_ref[...], two_ref[...])))
    )
    pl.when(pl.program_id(0) == 2)(
        lambda: out_ref.__setitem__(..., low(left_product(branch_ref[...], hid_ref[...])))
    )


def wide_products(after, mid_all, branch_all, two_low, hidden_low):
    return call(
        wide_kernel,
        [((WIDTH, 3 * WIDE), BF)],
        grid=(3,),
        in_specs=[
            ANY,
            pl.BlockSpec((GROUP, WIDTH), lambda i: (0, 0)),
            pl.BlockSpec((GROUP, WIDTH), lambda i: (0, 0)),
            pl.BlockSpec((GROUP, WIDE), lambda i: (0, jnp.minimum(i, 1))),
            pl.BlockSpec((GROUP, WIDE), lambda i: (0, 0)),
        ],
        out_specs=(pl.BlockSpec((WIDTH, WIDE), lambda i: (0, i)),),
    )(after, mid_all, branch_all, two_low, hidden_low)[0]


def attn_turn_kernel(*refs):
    pieces = refs[:4]
    mid_ref, dy_ref, g_ref, attn_ref, att_ref, inv_ref, w_ref = refs[4:11]
    grad_ref, pack_ref, prem_ref, term_ref = refs[11:]
    middle = mid_ref[...]
    gain = g_ref[2:3]
    back, term = normalize_back(middle, normalize(middle, gain)[1], gain, summed(pieces))
    prem_ref[...] = column_sum(term)
    middle_grad = dy_ref[...] + back
    grad_ref[...] = middle_grad
    attn_out = attn_ref[...]
    gain = g_ref[1:2]
    grad, term = normalize_back(attn_out, normalize(attn_out, gain)[1], gain, middle_grad)
    term_ref[...] = column_sum(term)
    attn_low = low(grad)
    pack_ref[:, :WIDTH] = attn_low
    both = low(product(attn_low, w_ref[...])).astype(F32) * att_ref[...]
    lane = lax.broadcasted_iota(jnp.int32, (OWN, 128), 1)
    inverse = inv_ref[...]
    high = low(inverse).astype(F32)
    stats = jnp.where(lane < HEADS, high, pltpu.roll(inverse - high, HEADS, 1))
    for h in range(HEADS):
        delta = jnp.sum(both[:, h * HEAD : (h + 1) * HEAD], axis=-1, keepdims=True)
        high = low(delta).astype(F32)
        stats = jnp.where(lane == 2 * HEADS + h, high, stats)
        stats = jnp.where(lane == 3 * HEADS + h, delta - high, stats)
    pack_ref[:, WIDTH:] = low(jnp.where(lane < 4 * HEADS, stats, 0.0))


def heads_up_kernel(*refs):
    pieces, (w_ref, all_ref, up_ref, stat_ref) = refs[:8], refs[8:]
    for j in range(8):
        for half in (0, 1):
            to = slice(256 * half + 32 * j, 256 * half + 32 * j + 32)
            own = slice(32 * half, 32 * half + 32)
            all_ref[to] = pieces[j][own, :WIDTH]
            stats = pieces[j][own, WIDTH:].astype(F32)
            stat_ref[to] = stats + pltpu.roll(stats, 128 - HEADS, 1)
    up_ref[...] = low(product(all_ref[...], w_ref[...]))


def backward_kernel(
    q_ref, kv_ref, place_ref, key_ref, up_ref, stat_ref, near_ref, far_ref, dkv_ref, all_ref, sum_ref
):
    at = place_ref[:, 0:1]
    start = place_ref[:, 1:2]
    pl.when(pl.program_id(0) == 0)(lambda: load_keys(kv_ref, all_ref))

    def part(count, first):
        spot = key_ref[:, :count]
        allowed = (spot <= at) & (spot >= start)
        keys = all_ref[:count, :HEAD]
        values = all_ref[:count, HEAD:]
        key_sum = jnp.zeros((count, HEAD), F32)
        value_sum = jnp.zeros((count, HEAD), F32)
        for h in range(HEADS):
            cols = slice(h * HEAD, (h + 1) * HEAD)
            query = q_ref[:, cols]
            up = up_ref[:, cols]
            scores = times_transpose(query, keys) * 0.0625
            probs = jnp.where(allowed, jnp.exp(scores), 0.0) * stat_ref[:, h : h + 1]
            probs_up = times_transpose(up, values)
            delta = stat_ref[:, 2 * HEADS + h : 2 * HEADS + h + 1]
            score_up = low(probs * (probs_up - delta))
            grad = low(product(score_up, keys) * 0.0625)
            near_ref[:, cols] = grad[:128]
            far_ref[:, cols] = grad[128:]
            key_sum = key_sum + left_product(score_up, query)
            value_sum = value_sum + left_product(low(probs), up)
        if first:
            sum_ref[:, :HEAD] = key_sum
            sum_ref[:, HEAD:] = value_sum
        else:
            half = KEYS // 2
            sides = (
                low((sum_ref[:, :HEAD] + key_sum[:half]) * 0.0625),
                low(sum_ref[:, HEAD:] + value_sum[:half]),
                low(key_sum[half:] * 0.0625),
                low(value_sum[half:]),
            )
            for i in range(16):
                own = slice(32 * i, 32 * i + 32)
                dkv_ref[i, :32, :HEAD] = sides[0][own]
                dkv_ref[i, :32, HEAD:] = sides[1][own]
                dkv_ref[i, 32:, :HEAD] = sides[2][own]
                dkv_ref[i, 32:, HEAD:] = sides[3][own]

    pl.when(pl.program_id(0) == 0)(lambda: part(KEYS // 2, True))
    pl.when(pl.program_id(0) == 1)(lambda: part(KEYS, False))


def attend_back(queries, keys_values, places, spots, upstream, stats):
    return call(
        backward_kernel,
        [((256, HEADS * HEAD), BF)] * 2 + [((16, OWN, 2 * HEAD), BF)],
        [pltpu.VMEM((KEYS, 2 * HEAD), BF), pltpu.VMEM((KEYS // 2, 2 * HEAD), F32)],
        grid=(2,),
        in_specs=[
            pl.BlockSpec((256, HEADS * HEAD), lambda i: (i, 0)),
            pl.BlockSpec((16, OWN, 2 * HEAD), lambda i: (0, 0, 0)),
            pl.BlockSpec((256, 2), lambda i: (i, 0)),
            pl.BlockSpec((1, KEYS), lambda i: (0, 0)),
            pl.BlockSpec((256, HEADS * HEAD), lambda i: (i, 0)),
            pl.BlockSpec((256, 128), lambda i: (i, 0)),
        ],
        out_specs=(
            pl.BlockSpec((128, HEADS * HEAD), lambda i: (i, 0)),
            pl.BlockSpec((128, HEADS * HEAD), lambda i: (i, 0)),
            pl.BlockSpec((16, OWN, 2 * HEAD), lambda i: (0, 0, 0)),
        ),
    )(queries, keys_values, places, spots, upstream, stats)


def lin_kernel(*refs):
    pieces = refs[:4]
    kv_ref, qlin_ref, klin_ref, cos_ref, sin_ref, gq_ref, gk_ref, att_ref = refs[4:12]
    out_ref, ql_ref, kl_ref, term_ref = refs[12:]
    kv_back = jnp.sum(kv_ref[...].astype(F32), axis=0)
    back = summed(pieces)
    cosine, sine = cos_ref[...], -sin_ref[...]
    key_lin = klin_ref[...]
    gain = gk_ref[...]
    grad, term = normalize_back(
        key_lin, normalize(key_lin, gain)[1], gain, turn(kv_back[:, :HEAD], cosine, sine)
    )
    term_ref[:, HEAD:] = column_sum(term)
    kv_low = low(jnp.concatenate([grad, kv_back[:, HEAD:]], axis=1))
    kl_ref[...] = kv_low
    gain = gq_ref[...]
    total = jnp.zeros((1, HEAD), F32)
    for h in range(HEADS):
        cols = slice(h * HEAD, (h + 1) * HEAD)
        lin = qlin_ref[:, cols]
        grad, term = normalize_back(
            lin, normalize(lin, gain)[1], gain, turn(back[:, cols], cosine, sine)
        )
        total = total + column_sum(term)
        query_low = low(grad)
        ql_ref[:, cols] = query_low
        heads = low(att_ref[:, cols])
        for zh in range(2):
            at = slice(zh * 128, zh * 128 + 128)
            out_ref[zh * 4 + h, :, :128] = query_low[:, at]
            out_ref[zh * 4 + h, :, 128:256] = heads[:, at]
            out_ref[zh * 4 + h, :, 256:] = kv_low[:, h * 128 + zh * 64 : h * 128 + zh * 64 + 64]
    term_ref[:, :HEAD] = total


def input_kernel(
    ql_ref, kl_ref, wq_ref, wkv_ref, x_ref, g_ref, mg_ref, t1, t2, t3, back_ref, out_ref, term_ref
):
    grad = times_transpose(ql_ref[...], wq_ref[...]) + times_transpose(kl_ref[...], wkv_ref[...])
    stream = x_ref[...]
    gain = g_ref[0:1]
    back, term = normalize_back(stream, normalize(stream, gain)[1], gain, grad)
    out_ref[...] = low(mg_ref[...] + back)
    terms = jnp.concatenate([column_sum(term), t1[...], t2[...], t3[...]] * 2, axis=0)
    rows = product(low(three_parts(terms)), back_ref[...])
    term_ref[...] = rows[:8] + rows[8:16] + rows[16:24]


def natural_kernel(mixed_ref, grad_ref, back_ref, out_ref):
    both = low(product(jnp.concatenate([mixed_ref[...], grad_ref[...]], axis=0), back_ref[...]))
    out_ref[:, :WIDTH] = both[:OWN]
    out_ref[:, WIDTH:] = both[OWN:]


def wide_out_kernel(z_ref, keep_ref, got_ref, gate_ref, up_ref, down_ref):
    for z in range(2):

        def place(z=z):
            pair = (keep_ref, got_ref) if z == 0 else (got_ref, keep_ref)
            for i, ref in enumerate((gate_ref, up_ref, down_ref)):
                cols = slice(i * WIDE, i * WIDE + HIDDEN)
                ref[...] = jnp.concatenate([half[:, cols].astype(F32) for half in pair], axis=1)

        pl.when(z_ref[0] == z)(place)


def narrow_kernel(after_ref, order_ref, lin_ref, normed_ref, attn_ref, gain_ref, out_ref, all_ref):
    for j in range(8):
        source = order_ref[j]
        all_ref[32 * j : 32 * j + 32] = lin_ref[source, :32]
        all_ref[256 + 32 * j : 288 + 32 * j] = lin_ref[source, 32:]
    normed = normed_ref[...]
    query = low(left_product(normed, all_ref[:, :128]))
    heads = low(left_product(attn_ref[...], all_ref[:, 128:256]))
    keys = low(left_product(normed, all_ref[:, 256:]))
    for i in range(16):
        own = slice(72 * i, 72 * i + 72)
        out_ref[i, :72, :128] = query[own]
        out_ref[i, :72, 128:256] = heads[own]
        out_ref[i, :72, 256:] = keys[own]
        out_ref[i, 72:, :] = gain_ref[...]


def per_device(
    hidden_in,
    cotangent,
    segment_ids,
    block_slot,
    w_query,
    w_key,
    w_value,
    w_out,
    w_gate,
    w_up,
    w_down,
    gain_in,
    gain_query,
    gain_key,
    gain_attn,
    gain_premlp,
    gain_mlpout,
):
    zh, at_x, at_y = lax.axis_index("zh"), lax.axis_index("x"), lax.axis_index("y")
    zl, core = lax.axis_index("zl"), lax.axis_index("c")
    shard = zl * 2 + core
    plane = at_x * 4 + at_y
    z = zh * 2 + zl
    place = jnp.asarray(INNER, jnp.int32)
    outer = low(place[:, None] == jnp.arange(WIDTH, dtype=jnp.int32)[None, :])
    inner = low(jnp.arange(WIDTH, dtype=jnp.int32)[:, None] == place[None, :])

    def by_zh(first, second):
        return jnp.where(zh == 0, first, second)

    both = jnp.concatenate([w_key, w_value], axis=1)
    quarter = lax.dynamic_slice_in_dim(both, shard * 128, 128, 1)
    pack = jnp.concatenate([w_query, quarter, w_out.T], axis=1)
    ring_pieces = [pack] + [ring(pack, step) for step in range(1, 4)]

    def four_heads(mine):
        other = swap(mine, "c")
        half = mine.shape[1] // 2
        first, second = jnp.where(core == 0, mine, other), jnp.where(core == 0, other, mine)
        return jnp.concatenate(
            [first[:, :half], second[:, :half], first[:, half:], second[:, half:]], axis=1
        )

    def whole(spread):
        return four_heads(spread.reshape(WIDTH, -1))

    spread_kv = spread_weights(256, 384, ring_pieces[3], z, ring_pieces)
    (out_block,) = call_after(
        lambda *refs: block_kernel(384, 640, *refs),
        [((72, 512), BF)],
        spread_kv,
        z.reshape(1),
        *ring_pieces,
        scalars=1,
    )
    full_out = lax.all_gather(four_heads(out_block), PLANE, axis=0, tiled=True)
    got_kv = plane_exchange(spread_kv)

    lead = jnp.sum((segment_ids < 1).astype(jnp.int32))
    tail = jnp.sum((segment_ids < 2).astype(jnp.int32))

    def start_of(index):
        return jnp.where(index >= tail, tail, jnp.where(index >= lead, lead, 0))

    step = jnp.arange(4, dtype=jnp.int32)
    from_z = (z - step) % 4
    near = jnp.where(
        from_z // 2 == 0,
        lax.dynamic_index_in_dim(block_slot, plane, 0, keepdims=False),
        lax.dynamic_index_in_dim(block_slot, 16 + plane, 0, keepdims=False),
    )
    flip = jnp.arange(2, dtype=jnp.int32)
    from_shard = (from_z % 2 * 2)[None, :] + jnp.where(flip == 0, core, 1 - core)[:, None]
    block = jnp.stack([near, 63 - near])[:, None, :]
    row = jnp.arange(32, dtype=jnp.int32)
    index = (block * 128 + from_shard[None] * 32)[..., None] + row
    index = index.reshape(GROUP)
    start = start_of(index)
    slots = lax.dynamic_slice_in_dim(block_slot, zh * 16, 16, 0)
    spots = jnp.stack([slots, 63 - slots])[:, :, None] * 128 + shard * 32 + row
    spots = spots.reshape(1, KEYS)
    places = jnp.stack([index, start], axis=1)
    freqs = THETA ** (-2.0 * jnp.arange(HEAD // 2, dtype=jnp.float32) / HEAD)
    angles = (index - start).astype(jnp.float32)[:, None] * freqs
    cosine, sine = jnp.cos(angles), jnp.sin(angles)

    def mine_of(rows):
        return rows.reshape(2, 8, 32, -1)[:, 0].reshape(OWN, -1)

    own_cosine, own_sine = mine_of(cosine), mine_of(sine)

    own_cosine, own_sine = mine_of(cosine), mine_of(sine)

    def four_rows(rows):
        flipped = swap(rows, "zl")
        mine = jnp.stack(
            [jnp.where(zl == 0, rows, flipped), jnp.where(zl == 0, flipped, rows)]
        )
        return mine, swap(mine, "c")

    def ordered(mine, other):
        rows = jnp.stack(
            [jnp.where(core == 0, mine, other), jnp.where(core == 0, other, mine)], axis=1
        )
        return jnp.moveaxis(rows.reshape(4, 2, 32, -1), 1, 0).reshape(256, -1)

    def take_own(rows):
        rows = lax.dynamic_index_in_dim(rows.reshape(2, 4, 32, WIDTH), shard, 1, keepdims=False)
        return rows.reshape(OWN, WIDTH)

    one = (1, WIDTH)
    stream, upstream, gains, normed_low = call_after(
        prepare_kernel,
        [((OWN, WIDTH), F32), ((OWN, WIDTH), F32), ((8, WIDTH), F32), ((OWN, WIDTH), BF)],
        spread_kv,
        take_own(hidden_in),
        take_own(cotangent),
        *[g.reshape(one) for g in (gain_in, gain_attn, gain_premlp, gain_mlpout)],
        inner,
    )
    gain_query, gain_key = gain_query.reshape(1, HEAD), gain_key.reshape(1, HEAD)
    keep, give = call_after(
        pack_kernel,
        [((ROWS, 3 * WIDE), BF)] * 2,
        spread_kv,
        zh.reshape(1),
        w_gate,
        w_up,
        w_down.T,
        scalars=1,
    )
    got_rows = swap(give, "zh")

    def copy_kernel(from_ref, to_ref):
        to_ref[...] = from_ref[...]

    (passed,) = call_after(copy_kernel, [((16, 72, 256), BF)], (got_rows, normed_low), got_kv)
    full_kv = whole(passed)

    def query_weights_kernel(*refs):
        weights_kernel(0, 256, *refs[:5], refs[6])
        refs[7][...] = refs[5][...]

    spread_query, normed_again = call_after(
        query_weights_kernel,
        [((16, 72, 512), BF), ((OWN, WIDTH), BF)],
        (got_kv, got_rows),
        z.reshape(1),
        *ring_pieces,
        normed_low,
        scalars=1,
    )
    got_query = plane_exchange(spread_query)
    full_query = whole(got_query)
    key_lin, spread_keys = call(key_kernel, [((OWN, HEAD), F32), ((16, OWN, 2 * HEAD), BF)])(
        normed_low, full_kv, gain_key,
        own_cosine,
        own_sine,
    )
    keys_values = plane_exchange(spread_keys)
    normed_pieces = gather_eight(normed_again)

    full = lax.all_gather(
        call_after(
            both_rows_kernel,
            [((72, 3 * WIDE), BF)],
            (got_query, full_out, spread_keys, *normed_pieces[5:]),
            zh.reshape(1),
            keep,
            got_rows,
            scalars=1,
        )[0],
        PLANE,
        axis=0,
        tiled=True,
    )

    normed_all, queries, query_lin = call(
        query_kernel,
        [((GROUP, WIDTH), BF), ((GROUP, HEADS * HEAD), BF), ((OWN, HEADS * HEAD), F32)],
    )(*normed_pieces, full_query, gain_query, cosine, sine)
    near, far = attend(queries, keys_values, places, spots)
    parts = scatter_eight(near, far, True, True)
    attended, attn_out, middle, mid_low, total_inv = call(
        middle_kernel,
        [
            ((OWN, HEADS * HEAD), F32),
            ((OWN, WIDTH), F32),
            ((OWN, WIDTH), F32),
            ((OWN, WIDTH), BF),
            ((OWN, 128), F32),
        ],
    )(*parts, full_out, stream, gains)

    mid_all, slope, act, hidden_low, near, far = call(
        hidden_kernel,
        [((GROUP, WIDTH), BF)] + [((GROUP, WIDE), BF)] * 3 + [((256, WIDTH), BF)] * 2,
    )(*gather_eight(mid_low), full)
    mixed, branch_low, mlpout_term = call(
        turning_kernel, [((OWN, WIDTH), BF), ((OWN, WIDTH), BF), (one, F32)]
    )(*scatter_eight(near, far, False), middle, upstream, gains)
    branch_all, two_low, near, far = call(
        hidden_back_kernel,
        [((GROUP, WIDTH), BF), ((GROUP, 2 * WIDE), BF)] + [((256, WIDTH), BF)] * 2,
    )(*gather_eight(branch_low), full, slope, act)
    parts = scatter_eight(near, far, False)
    wide_parts = wide_products(parts[0], mid_all, branch_all, two_low, hidden_low)
    wide = lax.psum_scatter(
        wide_parts,
        PLANE,
        scatter_dimension=0,
        tiled=True,
    )
    middle_grad, attn_pack, premlp_term, attn_term = call_after(
        attn_turn_kernel,
        [((OWN, WIDTH), F32), ((OWN, WIDTH + 128), BF), (one, F32), (one, F32)],
        wide_parts,
        *parts,
        middle,
        upstream,
        gains,
        attn_out,
        attended,
        total_inv,
        full_out,
    )
    attn_all, heads_up, stats = call(
        heads_up_kernel,
        [((GROUP, WIDTH), BF), ((GROUP, HEADS * HEAD), BF), ((GROUP, 128), F32)],
    )(
        *gather_eight(attn_pack),
        full_out,
    )
    near, far, kv_part = attend_back(queries, keys_values, places, spots, heads_up, stats)
    lin_parts, query_low, kv_low, head_terms = call(
        lin_kernel,
        [
            ((8, OWN, 320), BF),
            ((OWN, HEADS * HEAD), BF),
            ((OWN, 2 * HEAD), BF),
            ((1, 2 * HEAD), F32),
        ],
    )(
        *scatter_eight(near, far, True),
        plane_exchange(kv_part),
        query_lin,
        key_lin,
        own_cosine,
        own_sine,
        gain_query,
        gain_key,
        attended,
    )
    grad_own, terms = call(input_kernel, [((OWN, WIDTH), BF), ((8, WIDTH), F32)])(
        query_low,
        kv_low,
        full_query,
        full_kv,
        stream,
        gains,
        middle_grad,
        attn_term,
        premlp_term,
        mlpout_term,
        outer,
    )

    def by_rows(keep, give):
        got = swap(give, "zh")
        return by_zh(keep, got), by_zh(got, keep)

    order = (from_z[None, :] * 2 + jnp.where(flip == 0, core, 1 - core)[:, None]).reshape(8)
    sums = jnp.concatenate([terms[:4].reshape(-1), head_terms.reshape(-1)]).reshape(16, 320)
    keep_wide, give_wide = call(
        rows_kernel, [((ROWS, 3 * WIDE), BF)] * 2, in_specs=[SMEM, WHOLE]
    )(zh.reshape(1), wide)
    got_wide = swap(give_wide, "zh")
    (narrow,) = call(
        narrow_kernel,
        [((16, 104, 320), BF)],
        [pltpu.VMEM((GROUP, 320), BF)],
        in_specs=[ANY, SMEM] + [WHOLE] * 4,
    )(
        got_wide,
        order,
        lax.all_to_all(lin_parts, EIGHT, 0, 0),
        normed_all,
        attn_all,
        low(jnp.concatenate(split_two(sums), axis=0)),
    )
    outs = four_rows(
        call_after(natural_kernel, [((OWN, 2 * WIDTH), BF)], narrow, mixed, grad_own, outer)[0]
    )
    grad_gate, grad_up, grad_down = call_after(
        wide_out_kernel,
        [((ROWS, 2 * HIDDEN), F32)] * 3,
        narrow,
        zh.reshape(1),
        keep_wide,
        got_wide,
        scalars=1,
    )
    keep, give, sums = call_after(
        narrow_rows_kernel,
        [((ROWS, 320), BF)] * 2 + [((16, 320), F32)],
        (grad_gate, outs[0]),
        zh.reshape(1),
        plane_exchange(narrow),
        scalars=1,
    )
    narrow_pair = by_rows(keep, give)
    sums = sums + swap(sums, "c")
    sums = sums + ring(sums, 1) + ring(sums, 2) + ring(sums, 3)
    sums = sums.reshape(-1)

    def joined(pair, offset, width):
        return jnp.concatenate(
            [half[:, offset : offset + width] for half in pair], axis=1
        ).astype(F32)

    pair = narrow_pair
    grad_query = joined(pair, 0, 128)
    grad_out = joined(pair, 128, 128).T
    grad_kv = lax.all_gather(low(joined(pair, 256, 64)), ("zl", "c"), axis=1)
    grad_kv = grad_kv.reshape(ROWS, 2 * HEAD).astype(F32)

    rows = ordered(*outs)
    return (
        rows[:, :WIDTH],
        rows[:, WIDTH:].astype(F32),
        grad_query,
        grad_kv[:, :HEAD],
        grad_kv[:, HEAD:],
        grad_out,
        grad_gate,
        grad_up,
        grad_down.T,
        sums[:WIDTH],
        sums[4 * WIDTH : 4 * WIDTH + HEAD],
        sums[4 * WIDTH + HEAD :],
        sums[WIDTH : 2 * WIDTH],
        sums[2 * WIDTH : 3 * WIDTH],
        sums[3 * WIDTH : 4 * WIDTH],
    )


def solution(mesh):
    fine = Mesh(mesh.devices.reshape(2, 4, 4, 2, 2), ("zh", "x", "y", "zl", "c"))
    ctx, wt = ("zh", "x", "y"), ("zl", "c")
    rows, rows_wt, wt_rows = P(ctx, None), P(ctx, wt), P(wt, ctx)
    weights = (rows_wt, rows, rows, wt_rows, rows_wt, rows_wt, wt_rows)
    return jax.shard_map(
        per_device,
        mesh=fine,
        in_specs=(rows, rows, P(), P(), *weights, P(), P(), P(), P(), P(), P()),
        out_specs=(rows, rows, *weights, P(), P(), P(), P(), P(), P()),
        check_vma=False,
    )
```

```python
import jax
import jax.numpy as jnp
import numpy as np
from jax import lax
from jax.experimental import pallas as pl
from jax.experimental.pallas import tpu as pltpu
from jax.sharding import Mesh, PartitionSpec as P

EPSILON = 1e-06
THETA = 1000000.0
HEAD = 256
HEADS = 4
WIDTH = 1152
ROWS = 36
HIDDEN = 864
WIDE = 896
OWN = 64
GROUP = 512
KEYS = 1024
RING = ("zh", "zl")
EIGHT = ("zh", "zl", "c")
PLANE = ("x", "y")
VMEM_LIMIT = 56 * 1024 * 1024

_at = np.arange(WIDTH)
INNER = ((_at // ROWS) % 2 * 16 + (_at // ROWS) // 2) * ROWS + _at % ROWS


def normalize(values, gain):
    scale_inv = lax.rsqrt(jnp.mean(values * values, axis=-1, keepdims=True) + EPSILON)
    return (values * scale_inv * gain, scale_inv)


def normalize_back(values, scale_inv, gain, upstream):
    scaled = upstream * gain
    gain_term = upstream * values * scale_inv
    inner = jnp.mean(scaled * values, axis=-1, keepdims=True)
    return (scale_inv * scaled - values * scale_inv * scale_inv * scale_inv * inner, gain_term)


def turn(values, cosine, sine):
    half = values.shape[-1] // 2
    first = values[..., :half]
    second = values[..., half:]
    return jnp.concatenate(
        [first * cosine - second * sine, second * cosine + first * sine], axis=-1
    )


def product(left, right, **kw):
    return jnp.dot(left, right, preferred_element_type=jnp.float32, **kw)


def times_transpose(left, right, **kw):
    return lax.dot_general(
        left, right, (((1,), (1,)), ((), ())), preferred_element_type=jnp.float32, **kw
    )


def left_product(left, right):
    return lax.dot_general(
        left, right, (((0,), (0,)), ((), ())), preferred_element_type=jnp.float32
    )


def low(values):
    return values.astype(jnp.bfloat16)


def split_two(values):
    high = lax.reduce_precision(values, exponent_bits=8, mantissa_bits=7)
    return (high, values - high)


def swap(values, axis):
    return lax.ppermute(values, axis, [(0, 1), (1, 0)])


def ring(values, step):
    return lax.ppermute(values, RING, [(i, (i + step) % 4) for i in range(4)])


def call(body, outs, scratch=(), **kw):
    return pl.pallas_call(
        body,
        out_shape=tuple(jax.ShapeDtypeStruct(shape, kind) for shape, kind in outs),
        scratch_shapes=list(scratch),
        compiler_params=pltpu.CompilerParams(vmem_limit_bytes=VMEM_LIMIT),
        **kw,
    )


BF, F32 = jnp.bfloat16, jnp.float32
ANY = pl.BlockSpec(memory_space=pl.ANY)
SMEM = pl.BlockSpec(memory_space=pltpu.SMEM)
WHOLE = pl.BlockSpec(memory_space=pltpu.VMEM)


def call_after(body, outs, after, *args, scalars=0):
    after = after if isinstance(after, tuple) else (after,)
    return call(
        lambda *refs: body(*refs[len(after) :]),
        outs,
        in_specs=[ANY] * len(after) + [SMEM] * scalars + [WHOLE] * (len(args) - scalars),
    )(*after, *args)


def three_parts(values):
    high = low(values).astype(F32)
    mid = low(values - high).astype(F32)
    return jnp.concatenate([high, mid, values - high - mid], axis=0)


def gather_eight(piece):
    parts = [piece] + [ring(piece, step) for step in range(1, 4)]
    return parts + [swap(part, "c") for part in parts]


def add_split_kernel(totals, halves, a_ref, b_ref, *out_refs):
    both = a_ref[...].astype(F32) + b_ref[...].astype(F32)
    if totals:
        stats = both[:, 1024:]
        lane = lax.broadcasted_iota(jnp.int32, stats.shape, 1)
        summed = stats + pltpu.roll(stats, 128 - HEADS, 1)
        high = low(summed).astype(F32)
        rest = pltpu.roll(summed - high, HEADS, 1)
        stats = jnp.where(lane < HEADS, high, jnp.where(lane < 2 * HEADS, rest, 0.0))
        both = jnp.concatenate([both[:, :1024], stats], axis=1)
    both = low(both)
    for step in range(4):
        if halves:
            at = 32 * step
            out_refs[step][:32] = both[at : at + 32]
            out_refs[step][32:] = both[128 + at : 160 + at]
        else:
            out_refs[step][...] = both[64 * step : 64 * step + 64]


def scatter_eight(near, far, halves, totals=False):
    width = near.shape[-1]
    pieces = call(
        lambda *refs: add_split_kernel(totals, halves, *refs), [((OWN, width), BF)] * 4
    )(near, swap(far, "c"))
    return [pieces[0]] + [ring(pieces[step], -step) for step in range(1, 4)]


def summed(refs):
    total = refs[0][...].astype(F32)
    for ref in refs[1:]:
        total = total + ref[...].astype(F32)
    return total


def column_sum(term):
    return jnp.sum(term, axis=0, keepdims=True)


def prepare_kernel(own_ref, up_ref, gi_ref, ga_ref, gp_ref, gm_ref, inner_ref, x_ref, dy_ref, g_ref, n_ref):
    gains = [gi_ref[...], ga_ref[...], gp_ref[...], gm_ref[...]] * 2
    rows = [own_ref[...], up_ref[...], low(three_parts(jnp.concatenate(gains, axis=0)))]
    rows = product(jnp.concatenate(rows, axis=0), inner_ref[...])
    gains = rows[128:136] + rows[136:144] + rows[144:152]
    g_ref[...] = gains
    stream = rows[:OWN]
    x_ref[...] = stream
    dy_ref[...] = rows[OWN:128]
    n_ref[...] = low(normalize(stream, gains[0:1])[0])


def block_kernel(start, stop, z_ref, p0, p1, p2, p3, out_ref):
    pieces = (p0, p1, p2, p3)
    for z in range(4):

        def place(z=z):
            at = [pieces[(z - source) % 4][:, start:stop] for source in range(4)]
            out_ref[...] = jnp.concatenate(
                [jnp.concatenate(at[:2], axis=1), jnp.concatenate(at[2:], axis=1)], axis=0
            )

        pl.when(z_ref[0] == z)(place)


def weights_kernel(start, stop, z_ref, p0, p1, p2, p3, out_ref):
    pieces = (p0, p1, p2, p3)
    for z in range(4):

        def place(z=z):
            at = [pieces[(z - source) % 4][:, start:stop] for source in range(4)]
            block = jnp.concatenate(
                [jnp.concatenate(at[:2], axis=1), jnp.concatenate(at[2:], axis=1)], axis=0
            )
            for i in range(16):
                out_ref[i] = block

        pl.when(z_ref[0] == z)(place)


def spread_weights(start, stop, after, z, pieces):
    return call_after(
        lambda *refs: weights_kernel(start, stop, *refs),
        [((16, 72, 2 * (stop - start)), BF)],
        after,
        z.reshape(1),
        *pieces,
        scalars=1,
    )[0]


def pack_kernel(z_ref, gate_ref, up_ref, down_ref, keep_ref, give_ref):
    pad = jnp.zeros((ROWS, WIDE - HIDDEN), BF)
    for z in range(2):

        def place(z=z):
            for i, ref in enumerate((gate_ref, up_ref, down_ref)):
                rows = ref[...]
                sides = (rows[:, :HIDDEN], rows[:, HIDDEN:])
                cols = slice(i * WIDE, (i + 1) * WIDE)
                keep_ref[:, cols] = jnp.concatenate([sides[z], pad], axis=1)
                give_ref[:, cols] = jnp.concatenate([sides[1 - z], pad], axis=1)

        pl.when(z_ref[0] == z)(place)


def both_rows_kernel(z_ref, keep_ref, got_ref, out_ref):
    for z in range(2):

        def place(z=z):
            sides = (keep_ref[...], got_ref[...])
            out_ref[...] = jnp.concatenate([sides[z], sides[1 - z]], axis=0)

        pl.when(z_ref[0] == z)(place)


def rows_kernel(z_ref, got_ref, keep_ref, give_ref):
    for z in range(2):

        def place(z=z):
            grads = got_ref[...]
            sides = (grads[:ROWS], grads[ROWS:])
            keep_ref[...] = sides[z]
            give_ref[...] = sides[1 - z]

        pl.when(z_ref[0] == z)(place)


def narrow_rows_kernel(z_ref, got_ref, keep_ref, give_ref, sum_ref):
    total = jnp.sum(got_ref[...].astype(F32), axis=0)
    sum_ref[...] = total[72:88] + total[88:]
    for z in range(2):

        def place(z=z):
            sides = (low(total[:ROWS]), low(total[ROWS:72]))
            keep_ref[...] = sides[z]
            give_ref[...] = sides[1 - z]

        pl.when(z_ref[0] == z)(place)


def query_kernel(*refs):
    pieces, (w_ref, gain_ref, cos_ref, sin_ref, all_ref, q_ref, lin_ref) = refs[:8], refs[8:]
    for j in range(8):
        all_ref[32 * j : 32 * j + 32] = pieces[j][:32]
        all_ref[256 + 32 * j : 288 + 32 * j] = pieces[j][32:]
    rows = all_ref[...]
    for h in range(HEADS):
        cols = slice(h * HEAD, (h + 1) * HEAD)
        lin = product(rows, w_ref[:, cols])
        lin_ref[:32, cols] = lin[:32]
        lin_ref[32:, cols] = lin[256:288]
        q_ref[:, cols] = low(turn(normalize(lin, gain_ref[...])[0], cos_ref[...], sin_ref[...]))


def key_kernel(n_ref, w_ref, gain_ref, cos_ref, sin_ref, lin_ref, all_ref):
    lin = product(n_ref[...], w_ref[...])
    lin_ref[...] = lin[:, :HEAD]
    keys = turn(normalize(lin[:, :HEAD], gain_ref[...])[0], cos_ref[...], sin_ref[...])
    block = low(jnp.concatenate([keys, lin[:, HEAD:]], axis=1))
    for i in range(16):
        all_ref[i] = block


def plane_exchange(parts):
    return lax.all_to_all(parts, PLANE, 0, 0)


def load_keys(kv_ref, all_ref):
    for i in range(16):
        all_ref[32 * i : 32 * i + 32] = kv_ref[i, :32]
        all_ref[512 + 32 * i : 544 + 32 * i] = kv_ref[i, 32:]


def forward_kernel(q_ref, kv_ref, place_ref, key_ref, near_ref, far_ref, all_ref):
    at = place_ref[:, 0:1]
    start = place_ref[:, 1:2]
    pl.when(pl.program_id(0) == 0)(lambda: load_keys(kv_ref, all_ref))

    def part(count):
        spot = key_ref[:, :count]
        allowed = (spot <= at) & (spot >= start)
        keys = all_ref[:count, :HEAD]
        values = all_ref[:count, HEAD:]
        lane = lax.broadcasted_iota(jnp.int32, (256, 128), 1)
        stats = jnp.zeros((256, 128), F32)
        for h in range(HEADS):
            cols = slice(h * HEAD, (h + 1) * HEAD)
            scores = times_transpose(q_ref[:, cols], keys) * 0.0625
            expos = jnp.where(allowed, jnp.exp(scores), 0.0)
            total = jnp.sum(expos, axis=-1, keepdims=True)
            heads = low(product(low(expos), values))
            near_ref[:, cols] = heads[:128]
            far_ref[:, cols] = heads[128:]
            high = low(total).astype(F32)
            stats = jnp.where(lane == h, high, jnp.where(lane == HEADS + h, total - high, stats))
        near_ref[:, HEADS * HEAD :] = low(stats[:128])
        far_ref[:, HEADS * HEAD :] = low(stats[128:])

    pl.when(pl.program_id(0) == 0)(lambda: part(KEYS // 2))
    pl.when(pl.program_id(0) == 1)(lambda: part(KEYS))


def attend(queries, keys_values, places, spots):
    width = HEADS * HEAD + 128
    return call(
        forward_kernel,
        [((256, width), BF)] * 2,
        [pltpu.VMEM((KEYS, 2 * HEAD), BF)],
        grid=(2,),
        in_specs=[
            pl.BlockSpec((256, HEADS * HEAD), lambda i: (i, 0)),
            pl.BlockSpec((16, OWN, 2 * HEAD), lambda i: (0, 0, 0)),
            pl.BlockSpec((256, 2), lambda i: (i, 0)),
            pl.BlockSpec((1, KEYS), lambda i: (0, 0)),
        ],
        out_specs=(pl.BlockSpec((128, width), lambda i: (i, 0)),) * 2,
    )(queries, keys_values, places, spots)


def middle_kernel(*refs):
    pieces, (w_ref, x_ref, g_ref, att_ref, out_ref, mid_ref, n_ref, inv_ref) = refs[:4], refs[4:]
    reduced = summed(pieces)
    totals = reduced[:, 1024:] + pltpu.roll(reduced[:, 1024:], 128 - HEADS, 1)
    lane = lax.broadcasted_iota(jnp.int32, totals.shape, 1)
    inverse = 1.0 / jnp.where(lane < HEADS, totals, 1.0)
    inv_ref[...] = inverse
    attended = jnp.concatenate(
        [reduced[:, h * HEAD : (h + 1) * HEAD] * inverse[:, h : h + 1] for h in range(HEADS)], axis=1
    )
    att_ref[...] = attended
    attn_out = times_transpose(low(attended), w_ref[...])
    out_ref[...] = attn_out
    middle = x_ref[...] + normalize(attn_out, g_ref[1:2])[0]
    mid_ref[...] = middle
    n_ref[...] = low(normalize(middle, g_ref[2:3])[0])


ROOT = 0.7978845608028654


def hidden_kernel(*refs):
    pieces, (w_ref, all_ref, slope_ref, act_ref, hid_ref, near_ref, far_ref) = refs[:8], refs[8:]
    for j in range(8):
        all_ref[64 * j : 64 * j + 64] = pieces[j][...]
    for half, out_ref in ((0, near_ref), (1, far_ref)):
        own = slice(256 * half, 256 * half + 256)
        rows = all_ref[own]
        gate = product(rows, w_ref[:, :WIDE])
        up = product(rows, w_ref[:, WIDE : 2 * WIDE])
        square = gate * gate
        bend = jnp.tanh(ROOT * (gate + 0.044715 * square * gate))
        act = 0.5 * gate * (1.0 + bend)
        slope = 0.5 * (1.0 + bend) + 0.5 * gate * (1.0 - bend * bend) * (
            ROOT * (1.0 + 3.0 * 0.044715 * square)
        )
        slope_ref[own] = low(slope * up)
        act_ref[own] = low(act)
        hidden = low(act * up)
        hid_ref[own] = hidden
        out_ref[...] = low(times_transpose(hidden, w_ref[:, 2 * WIDE :]))


def turning_kernel(*refs):
    pieces, (mid_ref, dy_ref, g_ref, mixed_ref, low_ref, term_ref) = refs[:4], refs[4:]
    branch = summed(pieces)
    gain = g_ref[3:4]
    normed, scale = normalize(branch, gain)
    mixed_ref[...] = low(mid_ref[...] + normed)
    grad, term = normalize_back(branch, scale, gain, dy_ref[...])
    low_ref[...] = low(grad)
    term_ref[...] = column_sum(term)


def hidden_back_kernel(*refs):
    pieces, (w_ref, slope_ref, act_ref, all_ref, two_ref, near_ref, far_ref) = refs[:8], refs[8:]
    for j in range(8):
        all_ref[64 * j : 64 * j + 64] = pieces[j][...]
    for half, out_ref in ((0, near_ref), (1, far_ref)):
        own = slice(256 * half, 256 * half + 256)
        grad = product(all_ref[own], w_ref[:, 2 * WIDE :])
        gate = low(grad * slope_ref[own].astype(F32))
        up = low(grad * act_ref[own].astype(F32))
        two_ref[own, :WIDE] = gate
        two_ref[own, WIDE:] = up
        out_ref[...] = low(
            times_transpose(gate, w_ref[:, :WIDE]) + times_transpose(up, w_ref[:, WIDE : 2 * WIDE])
        )


def wide_kernel(after_ref, mid_ref, branch_ref, two_ref, hid_ref, out_ref):
    pl.when(pl.program_id(0) < 2)(
        lambda: out_ref.__setitem__(..., low(left_product(mid_ref[...], two_ref[...])))
    )
    pl.when(pl.program_id(0) == 2)(
        lambda: out_ref.__setitem__(..., low(left_product(branch_ref[...], hid_ref[...])))
    )


def wide_products(after, mid_all, branch_all, two_low, hidden_low):
    return call(
        wide_kernel,
        [((WIDTH, 3 * WIDE), BF)],
        grid=(3,),
        in_specs=[
            ANY,
            pl.BlockSpec((GROUP, WIDTH), lambda i: (0, 0)),
            pl.BlockSpec((GROUP, WIDTH), lambda i: (0, 0)),
            pl.BlockSpec((GROUP, WIDE), lambda i: (0, jnp.minimum(i, 1))),
            pl.BlockSpec((GROUP, WIDE), lambda i: (0, 0)),
        ],
        out_specs=(pl.BlockSpec((WIDTH, WIDE), lambda i: (0, i)),),
    )(after, mid_all, branch_all, two_low, hidden_low)[0]


def attn_turn_kernel(*refs):
    pieces = refs[:4]
    mid_ref, dy_ref, g_ref, attn_ref, att_ref, inv_ref, w_ref = refs[4:11]
    grad_ref, pack_ref, prem_ref, term_ref = refs[11:]
    middle = mid_ref[...]
    gain = g_ref[2:3]
    back, term = normalize_back(middle, normalize(middle, gain)[1], gain, summed(pieces))
    prem_ref[...] = column_sum(term)
    middle_grad = dy_ref[...] + back
    grad_ref[...] = middle_grad
    attn_out = attn_ref[...]
    gain = g_ref[1:2]
    grad, term = normalize_back(attn_out, normalize(attn_out, gain)[1], gain, middle_grad)
    term_ref[...] = column_sum(term)
    attn_low = low(grad)
    pack_ref[:, :WIDTH] = attn_low
    both = low(product(attn_low, w_ref[...])).astype(F32) * att_ref[...]
    lane = lax.broadcasted_iota(jnp.int32, (OWN, 128), 1)
    inverse = inv_ref[...]
    high = low(inverse).astype(F32)
    stats = jnp.where(lane < HEADS, high, pltpu.roll(inverse - high, HEADS, 1))
    for h in range(HEADS):
        delta = jnp.sum(both[:, h * HEAD : (h + 1) * HEAD], axis=-1, keepdims=True)
        high = low(delta).astype(F32)
        stats = jnp.where(lane == 2 * HEADS + h, high, stats)
        stats = jnp.where(lane == 3 * HEADS + h, delta - high, stats)
    pack_ref[:, WIDTH:] = low(jnp.where(lane < 4 * HEADS, stats, 0.0))


def heads_up_kernel(*refs):
    pieces, (w_ref, all_ref, up_ref, stat_ref) = refs[:8], refs[8:]
    for j in range(8):
        for half in (0, 1):
            to = slice(256 * half + 32 * j, 256 * half + 32 * j + 32)
            own = slice(32 * half, 32 * half + 32)
            all_ref[to] = pieces[j][own, :WIDTH]
            stats = pieces[j][own, WIDTH:].astype(F32)
            stat_ref[to] = stats + pltpu.roll(stats, 128 - HEADS, 1)
    up_ref[...] = low(product(all_ref[...], w_ref[...]))


def backward_kernel(
    q_ref, kv_ref, place_ref, key_ref, up_ref, stat_ref, near_ref, far_ref, dkv_ref, all_ref, sum_ref
):
    at = place_ref[:, 0:1]
    start = place_ref[:, 1:2]
    pl.when(pl.program_id(0) == 0)(lambda: load_keys(kv_ref, all_ref))

    def part(count, first):
        spot = key_ref[:, :count]
        allowed = (spot <= at) & (spot >= start)
        keys = all_ref[:count, :HEAD]
        values = all_ref[:count, HEAD:]
        key_sum = jnp.zeros((count, HEAD), F32)
        value_sum = jnp.zeros((count, HEAD), F32)
        for h in range(HEADS):
            cols = slice(h * HEAD, (h + 1) * HEAD)
            query = q_ref[:, cols]
            up = up_ref[:, cols]
            scores = times_transpose(query, keys) * 0.0625
            probs = jnp.where(allowed, jnp.exp(scores), 0.0) * stat_ref[:, h : h + 1]
            probs_up = times_transpose(up, values)
            delta = stat_ref[:, 2 * HEADS + h : 2 * HEADS + h + 1]
            score_up = low(probs * (probs_up - delta))
            grad = low(product(score_up, keys) * 0.0625)
            near_ref[:, cols] = grad[:128]
            far_ref[:, cols] = grad[128:]
            key_sum = key_sum + left_product(score_up, query)
            value_sum = value_sum + left_product(low(probs), up)
        if first:
            sum_ref[:, :HEAD] = key_sum
            sum_ref[:, HEAD:] = value_sum
        else:
            half = KEYS // 2
            sides = (
                low((sum_ref[:, :HEAD] + key_sum[:half]) * 0.0625),
                low(sum_ref[:, HEAD:] + value_sum[:half]),
                low(key_sum[half:] * 0.0625),
                low(value_sum[half:]),
            )
            for i in range(16):
                own = slice(32 * i, 32 * i + 32)
                dkv_ref[i, :32, :HEAD] = sides[0][own]
                dkv_ref[i, :32, HEAD:] = sides[1][own]
                dkv_ref[i, 32:, :HEAD] = sides[2][own]
                dkv_ref[i, 32:, HEAD:] = sides[3][own]

    pl.when(pl.program_id(0) == 0)(lambda: part(KEYS // 2, True))
    pl.when(pl.program_id(0) == 1)(lambda: part(KEYS, False))


def attend_back(queries, keys_values, places, spots, upstream, stats):
    return call(
        backward_kernel,
        [((256, HEADS * HEAD), BF)] * 2 + [((16, OWN, 2 * HEAD), BF)],
        [pltpu.VMEM((KEYS, 2 * HEAD), BF), pltpu.VMEM((KEYS // 2, 2 * HEAD), F32)],
        grid=(2,),
        in_specs=[
            pl.BlockSpec((256, HEADS * HEAD), lambda i: (i, 0)),
            pl.BlockSpec((16, OWN, 2 * HEAD), lambda i: (0, 0, 0)),
            pl.BlockSpec((256, 2), lambda i: (i, 0)),
            pl.BlockSpec((1, KEYS), lambda i: (0, 0)),
            pl.BlockSpec((256, HEADS * HEAD), lambda i: (i, 0)),
            pl.BlockSpec((256, 128), lambda i: (i, 0)),
        ],
        out_specs=(
            pl.BlockSpec((128, HEADS * HEAD), lambda i: (i, 0)),
            pl.BlockSpec((128, HEADS * HEAD), lambda i: (i, 0)),
            pl.BlockSpec((16, OWN, 2 * HEAD), lambda i: (0, 0, 0)),
        ),
    )(queries, keys_values, places, spots, upstream, stats)


def lin_kernel(*refs):
    pieces = refs[:4]
    kv_ref, qlin_ref, klin_ref, cos_ref, sin_ref, gq_ref, gk_ref, att_ref = refs[4:12]
    out_ref, ql_ref, kl_ref, term_ref = refs[12:]
    kv_back = jnp.sum(kv_ref[...].astype(F32), axis=0)
    back = summed(pieces)
    cosine, sine = cos_ref[...], -sin_ref[...]
    key_lin = klin_ref[...]
    gain = gk_ref[...]
    grad, term = normalize_back(
        key_lin, normalize(key_lin, gain)[1], gain, turn(kv_back[:, :HEAD], cosine, sine)
    )
    term_ref[:, HEAD:] = column_sum(term)
    kv_low = low(jnp.concatenate([grad, kv_back[:, HEAD:]], axis=1))
    kl_ref[...] = kv_low
    gain = gq_ref[...]
    total = jnp.zeros((1, HEAD), F32)
    for h in range(HEADS):
        cols = slice(h * HEAD, (h + 1) * HEAD)
        lin = qlin_ref[:, cols]
        grad, term = normalize_back(
            lin, normalize(lin, gain)[1], gain, turn(back[:, cols], cosine, sine)
        )
        total = total + column_sum(term)
        query_low = low(grad)
        ql_ref[:, cols] = query_low
        heads = low(att_ref[:, cols])
        for zh in range(2):
            at = slice(zh * 128, zh * 128 + 128)
            out_ref[zh * 4 + h, :, :128] = query_low[:, at]
            out_ref[zh * 4 + h, :, 128:256] = heads[:, at]
            out_ref[zh * 4 + h, :, 256:] = kv_low[:, h * 128 + zh * 64 : h * 128 + zh * 64 + 64]
    term_ref[:, :HEAD] = total


def input_kernel(
    ql_ref, kl_ref, wq_ref, wkv_ref, x_ref, g_ref, mg_ref, t1, t2, t3, back_ref, out_ref, term_ref
):
    grad = times_transpose(ql_ref[...], wq_ref[...]) + times_transpose(kl_ref[...], wkv_ref[...])
    stream = x_ref[...]
    gain = g_ref[0:1]
    back, term = normalize_back(stream, normalize(stream, gain)[1], gain, grad)
    out_ref[...] = low(mg_ref[...] + back)
    terms = jnp.concatenate([column_sum(term), t1[...], t2[...], t3[...]] * 2, axis=0)
    rows = product(low(three_parts(terms)), back_ref[...])
    term_ref[...] = rows[:8] + rows[8:16] + rows[16:24]


def natural_kernel(rows_ref, back_ref, out_ref):
    out_ref[...] = low(product(rows_ref[...], back_ref[...]))


def wide_out_kernel(z_ref, keep_ref, got_ref, gate_ref, up_ref, down_ref):
    for z in range(2):

        def place(z=z):
            pair = (keep_ref, got_ref) if z == 0 else (got_ref, keep_ref)
            for i, ref in enumerate((gate_ref, up_ref, down_ref)):
                cols = slice(i * WIDE, i * WIDE + HIDDEN)
                ref[...] = jnp.concatenate([half[:, cols].astype(F32) for half in pair], axis=1)

        pl.when(z_ref[0] == z)(place)


def narrow_kernel(after_ref, order_ref, lin_ref, normed_ref, attn_ref, gain_ref, out_ref, all_ref):
    for j in range(8):
        source = order_ref[j]
        all_ref[32 * j : 32 * j + 32] = lin_ref[source, :32]
        all_ref[256 + 32 * j : 288 + 32 * j] = lin_ref[source, 32:]
    normed = normed_ref[...]
    query = low(left_product(normed, all_ref[:, :128]))
    heads = low(left_product(attn_ref[...], all_ref[:, 128:256]))
    keys = low(left_product(normed, all_ref[:, 256:]))
    for i in range(16):
        own = slice(72 * i, 72 * i + 72)
        out_ref[i, :72, :128] = query[own]
        out_ref[i, :72, 128:256] = heads[own]
        out_ref[i, :72, 256:] = keys[own]
        out_ref[i, 72:, :] = gain_ref[...]


def per_device(
    hidden_in,
    cotangent,
    segment_ids,
    block_slot,
    w_query,
    w_key,
    w_value,
    w_out,
    w_gate,
    w_up,
    w_down,
    gain_in,
    gain_query,
    gain_key,
    gain_attn,
    gain_premlp,
    gain_mlpout,
):
    zh, at_x, at_y = lax.axis_index("zh"), lax.axis_index("x"), lax.axis_index("y")
    zl, core = lax.axis_index("zl"), lax.axis_index("c")
    shard = zl * 2 + core
    plane = at_x * 4 + at_y
    z = zh * 2 + zl
    place = jnp.asarray(INNER, jnp.int32)
    outer = low(place[:, None] == jnp.arange(WIDTH, dtype=jnp.int32)[None, :])
    inner = low(jnp.arange(WIDTH, dtype=jnp.int32)[:, None] == place[None, :])

    def by_zh(first, second):
        return jnp.where(zh == 0, first, second)

    both = jnp.concatenate([w_key, w_value], axis=1)
    quarter = lax.dynamic_slice_in_dim(both, shard * 128, 128, 1)
    pack = jnp.concatenate([w_query, quarter, w_out.T], axis=1)
    ring_pieces = [pack] + [ring(pack, step) for step in range(1, 4)]

    def four_heads(mine):
        other = swap(mine, "c")
        half = mine.shape[1] // 2
        first, second = jnp.where(core == 0, mine, other), jnp.where(core == 0, other, mine)
        return jnp.concatenate(
            [first[:, :half], second[:, :half], first[:, half:], second[:, half:]], axis=1
        )

    def whole(spread):
        return four_heads(spread.reshape(WIDTH, -1))

    spread_kv = spread_weights(256, 384, ring_pieces[3], z, ring_pieces)
    (out_block,) = call_after(
        lambda *refs: block_kernel(384, 640, *refs),
        [((72, 512), BF)],
        spread_kv,
        z.reshape(1),
        *ring_pieces,
        scalars=1,
    )
    full_out = lax.all_gather(four_heads(out_block), PLANE, axis=0, tiled=True)
    got_kv = plane_exchange(spread_kv)

    lead = jnp.sum((segment_ids < 1).astype(jnp.int32))
    tail = jnp.sum((segment_ids < 2).astype(jnp.int32))

    def start_of(index):
        return jnp.where(index >= tail, tail, jnp.where(index >= lead, lead, 0))

    step = jnp.arange(4, dtype=jnp.int32)
    from_z = (z - step) % 4
    near = jnp.where(
        from_z // 2 == 0,
        lax.dynamic_index_in_dim(block_slot, plane, 0, keepdims=False),
        lax.dynamic_index_in_dim(block_slot, 16 + plane, 0, keepdims=False),
    )
    flip = jnp.arange(2, dtype=jnp.int32)
    from_shard = (from_z % 2 * 2)[None, :] + jnp.where(flip == 0, core, 1 - core)[:, None]
    block = jnp.stack([near, 63 - near])[:, None, :]
    row = jnp.arange(32, dtype=jnp.int32)
    index = (block * 128 + from_shard[None] * 32)[..., None] + row
    index = index.reshape(GROUP)
    start = start_of(index)
    slots = lax.dynamic_slice_in_dim(block_slot, zh * 16, 16, 0)
    spots = jnp.stack([slots, 63 - slots])[:, :, None] * 128 + shard * 32 + row
    spots = spots.reshape(1, KEYS)
    places = jnp.stack([index, start], axis=1)
    freqs = THETA ** (-2.0 * jnp.arange(HEAD // 2, dtype=jnp.float32) / HEAD)
    angles = (index - start).astype(jnp.float32)[:, None] * freqs
    cosine, sine = jnp.cos(angles), jnp.sin(angles)

    def mine_of(rows):
        return rows.reshape(2, 8, 32, -1)[:, 0].reshape(OWN, -1)

    own_cosine, own_sine = mine_of(cosine), mine_of(sine)

    own_cosine, own_sine = mine_of(cosine), mine_of(sine)

    def four_rows(rows):
        flipped = swap(rows, "zl")
        mine = jnp.stack(
            [jnp.where(zl == 0, rows, flipped), jnp.where(zl == 0, flipped, rows)]
        )
        return mine, swap(mine, "c")

    def ordered(mine, other):
        rows = jnp.stack(
            [jnp.where(core == 0, mine, other), jnp.where(core == 0, other, mine)], axis=1
        )
        return jnp.moveaxis(rows.reshape(4, 2, 32, -1), 1, 0).reshape(256, -1)

    def take_own(rows):
        rows = lax.dynamic_index_in_dim(rows.reshape(2, 4, 32, WIDTH), shard, 1, keepdims=False)
        return rows.reshape(OWN, WIDTH)

    one = (1, WIDTH)
    stream, upstream, gains, normed_low = call_after(
        prepare_kernel,
        [((OWN, WIDTH), F32), ((OWN, WIDTH), F32), ((8, WIDTH), F32), ((OWN, WIDTH), BF)],
        spread_kv,
        take_own(hidden_in),
        take_own(cotangent),
        *[g.reshape(one) for g in (gain_in, gain_attn, gain_premlp, gain_mlpout)],
        inner,
    )
    gain_query, gain_key = gain_query.reshape(1, HEAD), gain_key.reshape(1, HEAD)
    keep, give = call_after(
        pack_kernel,
        [((ROWS, 3 * WIDE), BF)] * 2,
        spread_kv,
        zh.reshape(1),
        w_gate,
        w_up,
        w_down.T,
        scalars=1,
    )
    got_rows = swap(give, "zh")

    def copy_kernel(from_ref, to_ref):
        to_ref[...] = from_ref[...]

    (passed,) = call_after(copy_kernel, [((16, 72, 256), BF)], (got_rows, normed_low), got_kv)
    full_kv = whole(passed)

    def query_weights_kernel(*refs):
        weights_kernel(0, 256, *refs[:5], refs[6])
        refs[7][...] = refs[5][...]

    spread_query, normed_again = call_after(
        query_weights_kernel,
        [((16, 72, 512), BF), ((OWN, WIDTH), BF)],
        (got_kv, got_rows),
        z.reshape(1),
        *ring_pieces,
        normed_low,
        scalars=1,
    )
    got_query = plane_exchange(spread_query)
    full_query = whole(got_query)
    key_lin, spread_keys = call(key_kernel, [((OWN, HEAD), F32), ((16, OWN, 2 * HEAD), BF)])(
        normed_low, full_kv, gain_key,
        own_cosine,
        own_sine,
    )
    keys_values = plane_exchange(spread_keys)
    normed_pieces = gather_eight(normed_again)

    full = lax.all_gather(
        call_after(
            both_rows_kernel,
            [((72, 3 * WIDE), BF)],
            (got_query, full_out, spread_keys, *normed_pieces[5:]),
            zh.reshape(1),
            keep,
            got_rows,
            scalars=1,
        )[0],
        PLANE,
        axis=0,
        tiled=True,
    )

    normed_all, queries, query_lin = call(
        query_kernel,
        [((GROUP, WIDTH), BF), ((GROUP, HEADS * HEAD), BF), ((OWN, HEADS * HEAD), F32)],
    )(*normed_pieces, full_query, gain_query, cosine, sine)
    near, far = attend(queries, keys_values, places, spots)
    parts = scatter_eight(near, far, True, True)
    attended, attn_out, middle, mid_low, total_inv = call(
        middle_kernel,
        [
            ((OWN, HEADS * HEAD), F32),
            ((OWN, WIDTH), F32),
            ((OWN, WIDTH), F32),
            ((OWN, WIDTH), BF),
            ((OWN, 128), F32),
        ],
    )(*parts, full_out, stream, gains)

    mid_all, slope, act, hidden_low, near, far = call(
        hidden_kernel,
        [((GROUP, WIDTH), BF)] + [((GROUP, WIDE), BF)] * 3 + [((256, WIDTH), BF)] * 2,
    )(*gather_eight(mid_low), full)
    mixed, branch_low, mlpout_term = call(
        turning_kernel, [((OWN, WIDTH), BF), ((OWN, WIDTH), BF), (one, F32)]
    )(*scatter_eight(near, far, False), middle, upstream, gains)
    mixed_rows = four_rows(call(natural_kernel, [((OWN, WIDTH), BF)])(mixed, outer)[0])
    branch_all, two_low, near, far = call(
        hidden_back_kernel,
        [((GROUP, WIDTH), BF), ((GROUP, 2 * WIDE), BF)] + [((256, WIDTH), BF)] * 2,
    )(*gather_eight(branch_low), full, slope, act)
    parts = scatter_eight(near, far, False)
    wide_parts = wide_products(parts[0], mid_all, branch_all, two_low, hidden_low)
    wide = lax.psum_scatter(
        wide_parts,
        PLANE,
        scatter_dimension=0,
        tiled=True,
    )
    middle_grad, attn_pack, premlp_term, attn_term = call_after(
        attn_turn_kernel,
        [((OWN, WIDTH), F32), ((OWN, WIDTH + 128), BF), (one, F32), (one, F32)],
        wide_parts,
        *parts,
        middle,
        upstream,
        gains,
        attn_out,
        attended,
        total_inv,
        full_out,
    )
    attn_all, heads_up, stats = call_after(
        heads_up_kernel,
        [((GROUP, WIDTH), BF), ((GROUP, HEADS * HEAD), BF), ((GROUP, 128), F32)],
        mixed_rows[1],
        *gather_eight(attn_pack),
        full_out,
    )
    near, far, kv_part = attend_back(queries, keys_values, places, spots, heads_up, stats)
    lin_parts, query_low, kv_low, head_terms = call(
        lin_kernel,
        [
            ((8, OWN, 320), BF),
            ((OWN, HEADS * HEAD), BF),
            ((OWN, 2 * HEAD), BF),
            ((1, 2 * HEAD), F32),
        ],
    )(
        *scatter_eight(near, far, True),
        plane_exchange(kv_part),
        query_lin,
        key_lin,
        own_cosine,
        own_sine,
        gain_query,
        gain_key,
        attended,
    )
    grad_own, terms = call(input_kernel, [((OWN, WIDTH), BF), ((8, WIDTH), F32)])(
        query_low,
        kv_low,
        full_query,
        full_kv,
        stream,
        gains,
        middle_grad,
        attn_term,
        premlp_term,
        mlpout_term,
        outer,
    )

    def by_rows(keep, give):
        got = swap(give, "zh")
        return by_zh(keep, got), by_zh(got, keep)

    order = (from_z[None, :] * 2 + jnp.where(flip == 0, core, 1 - core)[:, None]).reshape(8)
    sums = jnp.concatenate([terms[:4].reshape(-1), head_terms.reshape(-1)]).reshape(16, 320)
    keep_wide, give_wide = call(
        rows_kernel, [((ROWS, 3 * WIDE), BF)] * 2, in_specs=[SMEM, WHOLE]
    )(zh.reshape(1), wide)
    got_wide = swap(give_wide, "zh")
    (narrow,) = call(
        narrow_kernel,
        [((16, 104, 320), BF)],
        [pltpu.VMEM((GROUP, 320), BF)],
        in_specs=[ANY, SMEM] + [WHOLE] * 4,
    )(
        got_wide,
        order,
        lax.all_to_all(lin_parts, EIGHT, 0, 0),
        normed_all,
        attn_all,
        low(jnp.concatenate(split_two(sums), axis=0)),
    )
    (grad_own,) = call_after(natural_kernel, [((OWN, WIDTH), BF)], narrow, grad_own, outer)
    grad_gate, grad_up, grad_down = call_after(
        wide_out_kernel,
        [((ROWS, 2 * HIDDEN), F32)] * 3,
        narrow,
        zh.reshape(1),
        keep_wide,
        got_wide,
        scalars=1,
    )
    keep, give, sums = call_after(
        narrow_rows_kernel,
        [((ROWS, 320), BF)] * 2 + [((16, 320), F32)],
        (grad_gate, grad_own),
        zh.reshape(1),
        plane_exchange(narrow),
        scalars=1,
    )
    narrow_pair = by_rows(keep, give)
    sums = sums + swap(sums, "c")
    sums = sums + ring(sums, 1) + ring(sums, 2) + ring(sums, 3)
    sums = sums.reshape(-1)

    def joined(pair, offset, width):
        return jnp.concatenate(
            [half[:, offset : offset + width] for half in pair], axis=1
        ).astype(F32)

    pair = narrow_pair
    grad_query = joined(pair, 0, 128)
    grad_out = joined(pair, 128, 128).T
    grad_kv = lax.all_gather(low(joined(pair, 256, 64)), ("zl", "c"), axis=1)
    grad_kv = grad_kv.reshape(ROWS, 2 * HEAD).astype(F32)

    rows = ordered(*four_rows(grad_own))
    return (
        ordered(*mixed_rows),
        rows.astype(F32),
        grad_query,
        grad_kv[:, :HEAD],
        grad_kv[:, HEAD:],
        grad_out,
        grad_gate,
        grad_up,
        grad_down.T,
        sums[:WIDTH],
        sums[4 * WIDTH : 4 * WIDTH + HEAD],
        sums[4 * WIDTH + HEAD :],
        sums[WIDTH : 2 * WIDTH],
        sums[2 * WIDTH : 3 * WIDTH],
        sums[3 * WIDTH : 4 * WIDTH],
    )


def solution(mesh):
    fine = Mesh(mesh.devices.reshape(2, 4, 4, 2, 2), ("zh", "x", "y", "zl", "c"))
    ctx, wt = ("zh", "x", "y"), ("zl", "c")
    rows, rows_wt, wt_rows = P(ctx, None), P(ctx, wt), P(wt, ctx)
    weights = (rows_wt, rows, rows, wt_rows, rows_wt, rows_wt, wt_rows)
    return jax.shard_map(
        per_device,
        mesh=fine,
        in_specs=(rows, rows, P(), P(), *weights, P(), P(), P(), P(), P(), P()),
        out_specs=(rows, rows, *weights, P(), P(), P(), P(), P(), P()),
        check_vma=False,
    )
```
